32 devices in a mesh: tok: 16 (over z, x, core), ch: 2 (over y).
Axes of the slice: x: 2, y: 2, z: 4, core: 2. Of those that a mesh axis runs over, the one named last changes fastest.
Arguments:
- tokens: bfloat16 [4096, 384], P(('tok', 'ch')), may hold values from -6 to 6
- cotangent: bfloat16 [4096, 384], P(('tok', 'ch')), may hold values from -6 to 6
- norm_gain: float32 [384], replicated, may hold values from 0.5 to 1.5
- in_proj: bfloat16 [384, 1536], replicated, may hold values from -0.3125 to 0.3125
- conv_weight: float32 [2, 4, 768], P(None, None, 'ch'), may hold values from -3 to 3
- conv_bias: float32 [2, 768], P(None, 'ch'), may hold values from -3 to 3
- select_proj: float32 [2, 768, 56], P(None, 'ch'), may hold values from -0.21875 to 0.21875
- step_proj: float32 [2, 24, 768], P(None, None, 'ch'), may hold values from -1.25 to 1.25
- step_bias: float32 [2, 768], P(None, 'ch'), may hold values from -5 to -2
- decay_log: float32 [2, 16, 768], P(None, None, 'ch'), may hold values from -5.3 to 0.7
- skip_gain: float32 [2, 768], P(None, 'ch'), may hold values from 0.5 to 1.5
- out_proj: bfloat16 [768, 384], P('ch'), may hold values from -0.4375 to 0.4375
- clip_lengths: int32 [16, 3], P('tok'), may hold values from 1 to 128, 256 in all within a row
Outputs:
- block_out: bfloat16 [4096, 384], P(('tok', 'ch'))
- grad_tokens: float32 [4096, 384], P(('tok', 'ch'))
- grad_gain: float32 [384], replicated
- grad_in_proj: float32 [384, 1536], replicated
- grad_conv_weight: float32 [2, 4, 768], P(None, None, 'ch')
- grad_conv_bias: float32 [2, 768], P(None, 'ch')
- grad_select_proj: float32 [2, 768, 56], P(None, 'ch')
- grad_step_proj: float32 [2, 24, 768], P(None, None, 'ch')
- grad_step_bias: float32 [2, 768], P(None, 'ch')
- grad_decay_log: float32 [2, 16, 768], P(None, None, 'ch')
- grad_skip_gain: float32 [2, 768], P(None, 'ch')
- grad_out_proj: float32 [768, 384], P('ch')
The draws below stay inside these ranges and needn't reach their ends.
Inputs may be any that keep to these rules, and one draw needn't show every extreme that they name: `clip_lengths`: each row gives the lengths of the 3 clips packed in order into one group of 256 tokens; a row sums to 256 and its longest clip has exactly 128 tokens.
All inputs are finite; a program needn't handle non-finite values.
Results may differ from the reference program's by a relative error of at most 0.01.
Values may be sent and summed in bfloat16 or wider, within the bound.
No kernel may reach another device: no remote copies, remote signals or barrier semaphores. Data moves between devices by JAX's collectives and lax.ppermute only.
A program may use at most 128 MiB of HBM per device.

```python
import math
import jax
import jax.numpy as jnp
import numpy as np
from jax import lax

D = 384
INNER = 768
STATE = 16
DT_RANK = 24
CONV = 4
GROUP = 256
TOKENS = 4096
XDBL = 56
LONGEST = 128
CLIPS = 3
N_TOK = 16


def shard_levels(rng, dims, pieces, least, top_value):
    gain = 1.0
    for dim, shards_of in pieces:
        heights = jax.random.uniform(jax.random.fold_in(jax.random.fold_in(rng, 6), dim), (shards_of,), jnp.float32, least / len(pieces), top_value / len(pieces))
        gain = gain * jnp.repeat(jnp.exp(heights), dims[dim] // shards_of).reshape((-1,) + (1,) * (len(dims) - 1 - dim))
    return gain


def split_up(amount, total, limit, slope):
    portions = [(1 << 20) // math.isqrt(standing ** slope) + 1 for standing in range(2, amount + 1)]
    rest, given = total - limit - (amount - 1), [1] * (amount - 1)
    while rest > 0:
        movable = [i for i in range(amount - 1) if given[i] < limit]
        pool, budget = sum([portions[i] for i in movable]), rest
        for i in movable:
            extra = min(limit - given[i], max(1, budget * portions[i] // pool), rest)
            given[i] = given[i] + extra
            rest = rest - extra
    return np.array([limit] + given)


def ragged_sizes(rng, count, total, limit, slope):
    if count == 2:
        one = jax.random.randint(rng, (), max(1, total - limit), min(limit, total - 1) + 1)
        return jnp.stack([one, total - one])
    tallies = jnp.asarray(split_up(count, total, limit, slope), jnp.int32)
    pairs = (count - 1) // 2
    donor, receiver = tallies[1:1 + 2 * pairs:2], tallies[2:2 + 2 * pairs:2]
    room = jnp.minimum(donor - 1, limit - receiver)
    moved = jax.random.randint(jax.random.fold_in(rng, 1), (pairs,), 0, 1 << 20) % (room + 1)
    tallies = tallies.at[1:1 + 2 * pairs:2].set(donor - moved).at[2:2 + 2 * pairs:2].set(receiver + moved)
    return tallies[jax.random.permutation(jax.random.fold_in(rng, 2), count)]


def scatter_about(own_key, extent, spread, reach, pieces=(), kind=jnp.bfloat16):
    gain = shard_levels(own_key, extent, pieces, -0.22, 0.18) if pieces else 1.0
    drawn = jax.random.normal(own_key, extent, jnp.float32) * spread * gain
    return jnp.minimum(jnp.maximum(drawn, -reach), reach).astype(kind)


def setup_inputs(seed: int = 0) -> dict:
    key_of = jax.random.split(jax.random.key(seed), 14)
    return {
        "tokens": scatter_about(key_of[0], (TOKENS, D), 1.0, 6.0, ((0, 32),)),
        "cotangent": scatter_about(key_of[1], (TOKENS, D), 1.0, 6.0, ((0, 32),)),
        "norm_gain": jnp.clip(1.0 + 0.1 * jax.random.normal(key_of[2], (D,), jnp.float32), 0.5, 1.5),
        "in_proj": scatter_about(key_of[3], (D, 2 * INNER), D ** -0.5, 0.3125),
        "conv_weight": scatter_about(key_of[4], (2, CONV, INNER), CONV ** -0.5, 3.0, ((2, 2),), jnp.float32),
        "conv_bias": scatter_about(key_of[5], (2, INNER), 0.5, 3.0, ((1, 2),), jnp.float32),
        "select_proj": scatter_about(key_of[6], (2, INNER, XDBL), INNER ** -0.5, 0.21875, ((1, 2),), jnp.float32),
        "step_proj": scatter_about(key_of[7], (2, DT_RANK, INNER), DT_RANK ** -0.5, 1.25, ((2, 2),), jnp.float32),
        "step_bias": jnp.clip(-5.0 + 3.0 * jax.random.uniform(key_of[8], (2, INNER), jnp.float32) ** shard_levels(key_of[8], (2, INNER), ((1, 2),), -0.2, 0.2), -5.0, -2.0),
        "decay_log": jnp.clip(-5.3 + 6 * jax.random.uniform(key_of[9], (2, STATE, INNER), jnp.float32) ** shard_levels(key_of[9], (2, STATE, INNER), ((2, 2),), -0.2, 0.2), -5.3, 0.7),
        "skip_gain": jnp.clip(0.5 + 1.0 * jax.random.uniform(key_of[10], (2, INNER), jnp.float32) ** shard_levels(key_of[10], (2, INNER), ((1, 2),), -0.2, 0.2), 0.5, 1.5),
        "out_proj": scatter_about(key_of[11], (INNER, D), (INNER // 4) ** -0.5, 0.4375, ((0, 2),)),
        "clip_lengths": jax.vmap(lambda own: ragged_sizes(own, CLIPS, GROUP, LONGEST, 2))(jax.random.split(key_of[12], N_TOK)).reshape((N_TOK, CLIPS)).astype(jnp.int32),
    }


norm_eps = 1e-05

@jax.custom_vjp
def low(v):
    return lax.optimization_barrier(v.astype(jnp.bfloat16)).astype(jnp.float32)

@jax.custom_vjp
def low_back(v):
    return v

def low_keep(v):
    return (low(v), None)

def low_pass(kept, grad):
    return (grad,)

def back_keep(v):
    return (v, None)

def back_low(kept, grad):
    return (low(grad),)
low.defvjp(low_keep, low_pass)
low_back.defvjp(back_keep, back_low)

def shift_rows(values, offset, fill_value):
    if offset == 0:
        return values
    filler = jnp.full((abs(offset),) + values.shape[1:], fill_value, values.dtype)
    if offset > 0:
        return jnp.concatenate([filler, values[:-offset]], axis=0)
    return jnp.concatenate([values[-offset:], filler], axis=0)

def clip_masks(lengths, length_total):
    clip_ends = jnp.cumsum(lengths).astype(jnp.int32)
    clip_starts = clip_ends - lengths
    position = jnp.arange(length_total, dtype=jnp.int32)
    starts_here = jnp.any(position[:, None] == clip_starts[None, :], axis=1)
    ends_here = jnp.any(position[:, None] == (clip_ends - 1)[None, :], axis=1)
    member = lax.optimization_barrier(jnp.sum((position[:, None] >= clip_ends[None, :]).astype(jnp.int32), axis=1))
    return (starts_here, ends_here, member)

def conv_silu(signal, conv_weight, conv_bias, member, direction_sign):
    tap_count = conv_weight.shape[0]
    summed = conv_bias[None, :] + jnp.zeros_like(signal)
    for lagged in range(tap_count):
        shifted = shift_rows(signal, direction_sign * lagged, 0.0)
        in_clip = shift_rows(member, direction_sign * lagged, -1) == member
        summed = summed + conv_weight[tap_count - 1 - lagged][None, :] * jnp.where(in_clip[:, None], shifted, 0.0)
    return jax.nn.silu(summed)

def combine_steps(earlier, latter):
    factor_one, added_one = earlier
    factor_two, added_two = latter
    return (factor_one * factor_two, factor_two * added_one + added_two)

def selective(activated, selected, step_proj, step_bias, decay_log, skip_gain, resets, reverse):
    rank_width = step_proj.shape[0]
    state_size = decay_log.shape[0]
    low_rank = selected[:, :rank_width]
    input_map = selected[:, rank_width:rank_width + state_size]
    output_map = selected[:, rank_width + state_size:]
    step_size = jax.nn.softplus(jnp.dot(low_rank, step_proj, precision=lax.Precision.HIGHEST) + step_bias[None, :])
    rates = -jnp.exp(decay_log)
    decays = jnp.exp(step_size[:, None, :] * rates[None, :, :])
    decays = jnp.where(resets[:, None, None], 0.0, decays)
    driving = (step_size * activated)[:, None, :] * input_map[:, :, None]
    _, states = lax.associative_scan(combine_steps, (decays, driving), reverse=reverse, axis=0)
    return lax.optimization_barrier(jnp.sum(states * output_map[:, :, None], axis=1)) + skip_gain[None, :] * activated

def direction(signal, conv_weight, conv_bias, select_proj, step_proj, step_bias, decay_log, skip_gain, member, resets, direction_sign, reverse):
    activated = conv_silu(signal, conv_weight, conv_bias, member, direction_sign)
    selected = jnp.dot(activated, select_proj, precision=lax.Precision.HIGHEST)
    return selective(activated, selected, step_proj, step_bias, decay_log, skip_gain, resets, reverse)

def forward(tokens, norm_gain, in_proj, conv_weight, conv_bias, select_proj, step_proj, step_bias, decay_log, skip_gain, out_proj, clip_lengths):
    scale_row = lax.rsqrt(lax.optimization_barrier(jnp.mean(tokens * tokens, axis=1, keepdims=True)) + norm_eps)
    normed = low(tokens * scale_row * norm_gain[None, :])
    projected = low_back(low(jnp.dot(normed, in_proj, precision=lax.Precision.HIGHEST)))
    group_count = clip_lengths.shape[0]
    inner_width = out_proj.shape[0]
    grouped = projected.reshape(group_count, -1, 2, inner_width)

    def one_group(items):
        block, lengths = items
        starts_here, ends_here, member = clip_masks(lengths, block.shape[0])
        signal = block[:, 0, :]
        gate_part = block[:, 1, :]
        ahead = direction(signal, conv_weight[0], conv_bias[0], select_proj[0], step_proj[0], step_bias[0], decay_log[0], skip_gain[0], member, starts_here, 1, False)
        behind = direction(signal, conv_weight[1], conv_bias[1], select_proj[1], step_proj[1], step_bias[1], decay_log[1], skip_gain[1], member, ends_here, -1, True)
        return (ahead + behind) * jax.nn.silu(gate_part) * 0.5
    gated = lax.map(jax.checkpoint(one_group), (grouped, clip_lengths))
    gated = low_back(low(gated.reshape(-1, inner_width)))
    return tokens + jnp.dot(gated, out_proj, precision=lax.Precision.HIGHEST)

def reference(tokens, cotangent, norm_gain, in_proj, conv_weight, conv_bias, select_proj, step_proj, step_bias, decay_log, skip_gain, out_proj, clip_lengths):
    primals = tuple((array_in.astype(jnp.float32) for array_in in (tokens, norm_gain, in_proj, conv_weight, conv_bias, select_proj, step_proj, step_bias, decay_log, skip_gain, out_proj)))

    def run_block(*inputs):
        return forward(*inputs, clip_lengths)
    block_out, pullback = jax.vjp(run_block, *primals)
    grad_tokens, grad_gain, grad_in_proj, grad_conv_weight, grad_conv_bias, grad_select_proj, grad_step_proj, grad_step_bias, grad_decay_log, grad_skip_gain, grad_out_proj = pullback(cotangent.astype(jnp.float32))
    return (block_out.astype(jnp.bfloat16), grad_tokens, grad_gain, grad_in_proj, grad_conv_weight, grad_conv_bias, grad_select_proj, grad_step_proj, grad_step_bias, grad_decay_log, grad_skip_gain, grad_out_proj)
```

```python
import functools
import math

import jax
import jax.numpy as jnp
import numpy as np
from jax import lax
from jax.experimental import pallas as pl
from jax.experimental.pallas import tpu as pltpu
from jax.sharding import PartitionSpec as P

norm_eps = 1e-05
F32 = jnp.float32
LOW = jnp.bfloat16
LANES = 128
HUGE_STEP = 1e30
LOG2E = math.log2(math.e)
LN2 = math.log(2.0)
BLOCK = 64
PAIRS = 8
PIECES = 4
FETCHES = 8


def mm(a, b):
    return lax.dot_general(a, b, (((1,), (0,)), ((), ())), preferred_element_type=F32)


def mm_nt(a, b):
    return lax.dot_general(a, b, (((1,), (1,)), ((), ())), preferred_element_type=F32)


def mm_tn(a, b):
    return lax.dot_general(a, b, (((0,), (0,)), ((), ())), preferred_element_type=F32)


def split(x):
    high = x.astype(LOW)
    return high, (x - high.astype(F32)).astype(LOW)


def mm3(dot, a, b):
    a_high, a_low = split(a)
    b_high, b_low = split(b)
    return dot(a_high, b_high) + (dot(a_high, b_low) + dot(a_low, b_high))


def round_up(x, m):
    return -(-x // m) * m


def wide(ref, *lead):
    parts = [ref[lead + (i,)] for i in range(ref.shape[len(lead)])]
    return parts[0] if len(parts) == 1 else jnp.concatenate(parts, axis=-1)


def row_time(r, length):
    return (r & 7) * length + (r >> 3)


def clip_places(len_ref, total, shape):
    t = row_time(lax.broadcasted_iota(jnp.int32, shape, 0), total // 8)
    clips = len_ref.shape[1]
    ends = []
    acc = 0
    for c in range(clips):
        acc = acc + len_ref[0, c]
        ends.append(acc)
    start = jnp.zeros(shape, jnp.int32)
    end = jnp.full(shape, total, jnp.int32)
    for c in range(clips - 1):
        start = jnp.where(t >= ends[c], ends[c], start)
    for c in range(clips - 2, -1, -1):
        end = jnp.where(t < ends[c], ends[c], end)
    return t - start, end - 1 - t


def order_matrix(first, rows, first_token, tokens, total):
    r = lax.broadcasted_iota(jnp.int32, (rows, tokens), 0) + first
    t = lax.broadcasted_iota(jnp.int32, (rows, tokens), 1) + first_token
    return jnp.where(row_time(r, total // 8) == t, 1.0, 0.0).astype(LOW)


def take_tokens(first, rows, total):
    t = lax.broadcasted_iota(jnp.int32, (rows, total), 0) + first
    r = lax.broadcasted_iota(jnp.int32, (rows, total), 1)
    return jnp.where(row_time(r, total // 8) == t, 1.0, 0.0).astype(LOW)


def halo_fill(ext_ref, total, halo, sl):
    for q in range(halo // 8):
        tail = ext_ref[pl.ds(total + 8 * q, 8), sl]
        ext_ref[pl.ds(8 * q, 8), sl] = pltpu.roll(tail, 1, 0)
        head = ext_ref[pl.ds(halo + 8 * q, 8), sl]
        ext_ref[pl.ds(halo + total + 8 * q, 8), sl] = pltpu.roll(head, 7, 0)


def link_blocks(gain, added, toward_end):
    row = lax.broadcasted_iota(jnp.int32, gain.shape, 0)
    for k in (1, 2, 4):
        shift = k if toward_end else 8 - k
        inside = (row >= k) if toward_end else (row < 8 - k)
        added_near = jnp.where(inside, pltpu.roll(added, shift, 0), 0.0)
        gain_near = jnp.where(inside, pltpu.roll(gain, shift, 0), 1.0)
        added = added + gain * added_near
        gain = gain * gain_near
    if toward_end:
        return jnp.where(row >= 1, pltpu.roll(added, 1, 0), 0.0)
    return jnp.where(row < 7, pltpu.roll(added, 7, 0), 0.0)


def over_rows(total, body):
    def step(i, carry):
        body(pl.multiple_of(i * BLOCK, BLOCK))
        return carry

    lax.fori_loop(0, total // BLOCK, step, 0)


def over_pairs(length, body, init):
    def trip(i, carry):
        for q in range(PAIRS):
            carry = body(i * PAIRS + q, carry)
        return carry

    return lax.fori_loop(0, length // 2 // PAIRS, trip, init)


def tile(lt):
    return slice(lt * LANES, (lt + 1) * LANES)


def lane(n):
    return slice(n * LANES, (n + 1) * LANES)


def sigmoid(x):
    return 0.5 * jnp.tanh(0.5 * x) + 0.5


def fetch_all(sources, targets, sems):
    copies = [pltpu.make_async_copy(a, b, sems.at[i]) for i, (a, b) in enumerate(zip(sources, targets))]
    for copy in copies:
        copy.start()
    return copies


def weight_kernel(dims, select_hbm, taps_hbm, bias_hbm, packed_ref, select_ref, taps_ref, bias_ref, sems):
    taps, real = taps_ref.shape[1:]
    xd = select_ref.shape[1]
    for copy in fetch_all((select_hbm, taps_hbm, bias_hbm), (select_ref, taps_ref, bias_ref), sems):
        copy.wait()
    parts = [select_ref[0], select_ref[1], jnp.zeros((LANES - 2 * xd, real), F32)]
    packed_ref[0:LANES, 0:real] = jnp.concatenate(parts, axis=0).astype(LOW)
    parts = []
    for d in range(2):
        parts += [taps_ref[d], bias_ref[d:d + 1, :]]
    parts.append(jnp.zeros((16 - 2 * (taps + 1), real), F32))
    high, low = split(jnp.concatenate(parts, axis=0))
    packed_ref[LANES:LANES + 16, 0:real] = high
    packed_ref[LANES + 16:LANES + 32, 0:real] = low
    if real < packed_ref.shape[1]:
        packed_ref[:, real:] = jnp.zeros((LANES + 32, packed_ref.shape[1] - real), LOW)


def fetch_kernel(n, *refs):
    sources, targets, sems = refs[:n], refs[n + 1:2 * n + 1], refs[-1]
    rows = sources[0].shape[0] // FETCHES
    parts = [pl.ds(i * rows, rows) for i in range(FETCHES)]
    for copy in fetch_all(
        [sources[0].at[part, :] for part in parts] + list(sources[1:]),
        [targets[0].at[part, :] for part in parts] + list(targets[1:]), sems,
    ):
        copy.wait()


def norm_kernel(dims, len_hbm, own_ref, gain_ref, win_ref, *refs):
    n_ch, n_tok, rows, width, chans, inner, rank, states, taps = dims
    total = rows * n_ch
    toks = [own_ref, *refs[:n_ch - 1]]
    normed_ref, xp_ref, sigs_ref, gate_ref, pos_ref, rem_ref, len_ref, sem = refs[n_ch - 1:]
    me = lax.axis_index("ch")
    fetch = pltpu.make_async_copy(len_hbm, len_ref, sem)
    fetch.start()
    gain = gain_ref[...][None, :]
    for r0 in range(0, total, 256):
        rr = slice(r0, r0 + 256)
        xp = 0.0
        for k in range(n_ch):
            xp = xp + mm(order_matrix(r0, 256, lax.rem(me + k, n_ch) * rows, rows, total), toks[k][...])
        xp_ref[rr, :] = xp.astype(LOW)
        scale = lax.rsqrt(jnp.mean(xp * xp, axis=1, keepdims=True) + norm_eps)
        normed_ref[rr, :] = (xp * scale * gain).astype(LOW)
    normed = normed_ref[...]
    for k in range(n_ch):
        j = lax.rem(me + k, n_ch)
        sigs_ref[k] = mm(normed, win_ref[:, pl.ds(pl.multiple_of(j * chans, LANES), chans)]).astype(LOW)
    gate_ref[...] = mm(
        normed, win_ref[:, pl.ds(pl.multiple_of(inner + me * chans, LANES), chans)]
    ).astype(LOW)
    fetch.wait()
    pos, rem = clip_places(len_ref, total, (total, LANES))
    pos_ref[...] = pos
    rem_ref[...] = rem


def conv_silu(dims, k, sigs_ref, pack_ref, pos_ref, rem_ref, act_refs, dsil_refs, ext_ref):
    n_ch, n_tok, rows, width, chans, inner, rank, states, taps = dims
    total = rows * n_ch
    halo = 8 * (taps - 1)
    ext_ref[pl.ds(halo, total), :] = sigs_ref[k].astype(F32)
    halo_fill(ext_ref, total, halo, slice(None))
    conv = conv_rows_of(pack_ref, taps)

    def conv_rows(r0):
        pos_b = pos_ref[pl.ds(r0, BLOCK), :]
        rem_b = rem_ref[pl.ds(r0, BLOCK), :]
        for lt in range(chans // LANES):
            sl = tile(lt)
            for d in range(2):
                inside = rem_b if d else pos_b
                at = d * (taps + 1)
                summed = conv[at + taps:at + taps + 1, sl] + conv[at + taps - 1:at + taps, sl] * ext_ref[
                    pl.ds(r0 + halo, BLOCK), sl
                ]
                for lag in range(1, taps):
                    far = ext_ref[pl.ds(r0 + (halo + 8 * lag if d else halo - 8 * lag), BLOCK), sl]
                    summed = summed + conv[at + taps - 1 - lag:at + taps - lag, sl] * jnp.where(
                        inside >= lag, far, 0.0
                    )
                sg = sigmoid(summed)
                active = summed * sg
                act_refs[d][lt, pl.ds(r0, BLOCK), :] = active
                if dsil_refs is not None:
                    dsil_refs[d][lt, pl.ds(r0, BLOCK), :] = sg + active * (1.0 - sg)

    over_rows(total, conv_rows)
    out = []
    for d in range(2):
        high, low = split(wide(act_refs[d]))
        sel = pack_ref[0:LANES, :]
        out.append(mm_nt(high, sel) + mm_nt(low, sel))
    return out


def own_front_kernel(dims, pack_ref, sigs_ref, pos_ref, rem_ref, act0_ref, act1_ref, dsil0_ref, dsil1_ref, part_ref,
                     ext_ref):
    parts = conv_silu(dims, 0, sigs_ref, pack_ref, pos_ref, rem_ref, (act0_ref, act1_ref), (dsil0_ref, dsil1_ref),
                      ext_ref)
    for d in range(2):
        part_ref[d] = parts[d]


def front_kernel(dims, *refs):
    n_ch, n_tok, rows, width, chans, inner, rank, states, taps = dims
    total = rows * n_ch
    nt = chans // LANES
    xd = rank + 2 * states
    packs = refs[:n_ch - 1]
    (sigs_ref, pos_ref, rem_ref, part_ref, stepw_hbm, sbias_hbm, picked_ref, stp0_ref, stp1_ref, sgm0_ref, sgm1_ref,
     ext_ref, stepw_pad_ref, pre_ref, act0_ref, act1_ref, stepw_ref, sbias_ref, sems) = refs[n_ch - 1:]
    stp_refs, sgm_refs = (stp0_ref, stp1_ref), (sgm0_ref, sgm1_ref)
    fetches = fetch_all((stepw_hbm, sbias_hbm), (stepw_ref, sbias_ref), sems)
    picked_ref[...] = part_ref[...]
    for k in range(1, n_ch):
        parts = conv_silu(dims, k, sigs_ref, packs[k - 1], pos_ref, rem_ref, (act0_ref, act1_ref), None, ext_ref)
        for d in range(2):
            picked_ref[d] += parts[d]
    for fetch in fetches:
        fetch.wait()
    stepw_pad_ref[...] = jnp.zeros_like(stepw_pad_ref)
    for d in range(2):
        base = d * xd
        stepw_pad_ref[d, base:base + rank, :] = stepw_ref[d]
        pre_ref[...] = mm3(mm, picked_ref[d], stepw_pad_ref[d]) + sbias_ref[d:d + 1, :]

        def step_rows(r0):
            for lt in range(nt):
                x = pre_ref[pl.ds(r0, BLOCK), tile(lt)]
                tail = jnp.exp(-jnp.abs(x))
                whole = 1.0 + tail
                inv = pltpu.reciprocal(whole, approx=True)
                inv = inv * (2.0 - whole * inv)
                small = tail * (1.0 - tail * (0.5 - tail * (1.0 / 3.0)))
                stp_refs[d][lt, pl.ds(r0, BLOCK), :] = jnp.maximum(x, 0.0) + jnp.where(
                    tail < 1e-3, small, jnp.log(whole)
                )
                sgm_refs[d][lt, pl.ds(r0, BLOCK), :] = jnp.where(x >= 0.0, inv, tail * inv)

        over_rows(total, step_rows)


def conv_rows_of(pack_ref, taps):
    return pack_ref[LANES:LANES + 16, :].astype(F32) + pack_ref[LANES + 16:LANES + 32, :].astype(F32)


def selectors(states):
    lanes = np.arange(states * LANES) >> 7
    column = np.arange(LANES)
    spread = ((column[:, None] % states) == lanes[None, :]) & (column[:, None] < 2 * states)
    gather = lanes[:, None] == column[None, :]
    return jnp.asarray(spread, LOW), jnp.asarray(gather, LOW)


def spread_maps(first, states, picked, lanes_ref, e_ref, dest):
    moved = pltpu.roll(picked, LANES - first, 1)
    high = moved.astype(LOW).astype(F32)
    low = pltpu.roll(moved - high, states, 1)
    spot = lax.broadcasted_iota(jnp.int32, moved.shape, 1)
    lanes_ref[...] = jnp.where(spot < states, high, jnp.where(spot < 2 * states, low, 0.0)).astype(LOW)

    dest[...] = mm(lanes_ref[...], e_ref[...])


def fill_rates(rate, nt, states, r2_ref):
    for lt in range(nt):
        for n in range(states):
            r2_ref[lt, n] = jnp.broadcast_to(rate[n:n + 1, tile(lt)] * LOG2E, (8, LANES))


def gate_kernel(dims, *refs):
    n_ch, n_tok, rows, width, chans, inner, rank, states, taps = dims
    total = rows * n_ch
    cots = refs[:n_ch]
    wout_ref, gate_ref, _, cotp_ref, gg_ref, gy_ref = refs[n_ch:]
    me = lax.axis_index("ch")
    for r0 in range(0, total, 256):
        cotp = 0.0
        for k in range(n_ch):
            moved = order_matrix(r0, 256, lax.rem(me + k, n_ch) * rows, rows, total)
            cotp = cotp + mm(moved, cots[k][...])
        cotp_ref[r0:r0 + 256, :] = cotp.astype(LOW)
    gg_ref[...] = mm_nt(cotp_ref[...], wout_ref[...]).astype(LOW)

    def gate_rows(r0):
        rr = pl.ds(r0, BLOCK)
        for lt in range(chans // LANES):
            gate = gate_ref[rr, tile(lt)].astype(F32)
            gy_ref[lt, rr, :] = gg_ref[rr, tile(lt)].astype(F32) * (gate * sigmoid(gate)) * 0.5

    over_rows(total, gate_rows)


def forward_kernel(dims, d, gy_ref, act_ref, stp_ref, picked_ref, dlog_ref, place_ref, e_ref, er_ref, *refs):
    n_ch, n_tok, rows, width, chans, inner, rank, states, taps = dims
    total = rows * n_ch
    length = total // 8
    nt = chans // LANES
    xd = rank + 2 * states
    first = d * xd + rank
    (y_ref, gains_ref, bb_ref, cb_ref, a_ref, h_ref, gmap_ref,
     r2_ref, lanes_ref, p_ref) = refs
    zero = jnp.zeros((8, LANES), F32)
    fill_rates(-jnp.exp(dlog_ref[d]), nt, states, r2_ref)
    spread_maps(first, states, picked_ref[d], lanes_ref, e_ref, bb_ref)
    spread_maps(first + states, states, picked_ref[d], lanes_ref, e_ref, cb_ref)
    p_ref[...] = jnp.zeros_like(p_ref)

    def along(j):
        return pl.multiple_of((length - 1 - j if d else j) * 8, 8)

    def scan_tile(lt, carry):
        def ends(j2, state):
            state, step_sum = list(state[:-1]), state[-1]
            at = [along(2 * j2 + jj) for jj in range(2)]
            sk, u = [], []
            for r0 in at:
                step = stp_ref[lt, pl.ds(r0, 8), :]
                sk.append(jnp.where(place_ref[pl.ds(r0, 8), :] == 0, HUGE_STEP, step))
                u.append(step * act_ref[lt, pl.ds(r0, 8), :])
            for n in range(states):
                for jj, r0 in enumerate(at):
                    a = jnp.exp2(sk[jj] * r2_ref[lt, n])
                    a_ref[lt, pl.ds(r0, 8), lane(n)] = a
                    state[n] = a * state[n] + u[jj] * bb_ref[pl.ds(r0, 8), lane(n)]
            return tuple(state) + (step_sum + (sk[0] + sk[1]),)

        out = over_pairs(length, ends, (zero,) * (states + 1))
        begin = []
        for n in range(states):
            whole_gain = jnp.exp2(out[-1] * r2_ref[lt, n])
            gains_ref[lt, n] = whole_gain
            begin.append(link_blocks(whole_gain, out[n], d == 0))

        def forward(j2, state):
            state = list(state)
            at = [along(2 * j2 + jj) for jj in range(2)]
            r16 = pl.multiple_of((length - 2 - 2 * j2 if d else 2 * j2) * 8, 16)
            u = [stp_ref[lt, pl.ds(r0, 8), :] * act_ref[lt, pl.ds(r0, 8), :] for r0 in at]
            gy = [gy_ref[lt, pl.ds(r0, 8), :] for r0 in at]
            sums = [[None, None], [None, None]]
            for n in range(states):
                prods = []
                for jj, r0 in enumerate(at):
                    h_ref[lt, pl.ds(r0, 8), lane(n)] = state[n]
                    state[n] = a_ref[lt, pl.ds(r0, 8), lane(n)] * state[n] + u[jj] * bb_ref[pl.ds(r0, 8), lane(n)]
                    term = state[n] * cb_ref[pl.ds(r0, 8), lane(n)]
                    sums[jj][n % 2] = term if sums[jj][n % 2] is None else sums[jj][n % 2] + term
                    prods.append(state[n] * gy[jj])
                p_ref[pl.ds(r16, 16), lane(n)] += jnp.concatenate(prods[::-1] if d else prods, axis=0).astype(LOW)
            for jj, r0 in enumerate(at):
                y_ref[lt, pl.ds(r0, 8), :] = sums[jj][0] + sums[jj][1]
            return tuple(state)

        over_pairs(length, forward, tuple(begin))
        return carry

    lax.fori_loop(0, nt, scan_tile, 0)
    gmap_ref[...] = pltpu.roll(mm(p_ref[...], er_ref[...]), first + states, 1)


def out_kernel(dims, y0_ref, y1_ref, act0_ref, act1_ref, skip_ref, gate_ref, gg_ref, normed_ref, cotp_ref, *refs):
    n_ch, n_tok, rows, width, chans, inner, rank, states, taps = dims
    total = rows * n_ch
    gated_ref, ggate_ref, own_ref, send_ref = refs

    def gate_back(r0):
        rr = pl.ds(r0, BLOCK)
        for lt in range(chans // LANES):
            sl = tile(lt)
            out = (
                y0_ref[lt, rr, :] + y1_ref[lt, rr, :]
                + skip_ref[0:1, sl] * act0_ref[lt, rr, :] + skip_ref[1:2, sl] * act1_ref[lt, rr, :]
            ) * 0.5
            gate = gate_ref[rr, sl].astype(F32)
            sg = sigmoid(gate)
            silu = gate * sg
            gated_ref[rr, sl] = (out * silu).astype(LOW)
            ggate_ref[rr, sl] = (gg_ref[rr, sl].astype(F32) * out * (sg + silu * (1.0 - sg))).astype(LOW)

    over_rows(total, gate_back)
    gated = gated_ref[...]
    gout = mm_tn(gated, cotp_ref[...])
    gin = mm_tn(normed_ref[...], ggate_ref[...])
    folded = [gout[:, i * chans:(i + 1) * chans] for i in range(width // chans)]
    pack(own_ref, send_ref, [folded, [gin]])


def block_kernel(dims, gated_ref, wout_ref, _, own_ref, *refs):
    n_ch, rows = dims[0], dims[2]
    part = mm(gated_ref[...], wout_ref[...])
    token_rows(lax.axis_index("ch"), part, n_ch, rows, rows * n_ch, own_ref, refs)


def token_rows(me, part, n_ch, rows, total, own_ref, other_refs):
    high, low = split(part)
    mine = take_tokens(me * rows, rows, total)
    own_ref[...] = mm(mine, high) + mm(mine, low)
    for k in range(1, n_ch):
        theirs = take_tokens(lax.rem(me + k, n_ch) * rows, rows, total)
        other_refs[k - 1][...] = mm(theirs, high).astype(LOW)


def my_place():
    tok = lax.axis_index("tok")
    return tok & 1, (tok >> 1) & 1


def pack(own_ref, send_ref, groups):
    core, near = my_place()
    runs = []
    at = 0
    for group in groups:
        total = sum(piece.shape[0] for piece in group)
        size = chunk_rows(PIECES, total)
        place = 0
        for piece in group:
            for i in range(0, piece.shape[0], 8):
                runs.append(divmod(place + i, size) + (at, piece[i:i + 8, :]))
            place += piece.shape[0]
        for i in range(place, size * PIECES, 8):
            runs.append(divmod(i, size) + (at, jnp.zeros((8, own_ref.shape[2]), F32)))
        at += size
    for side in range(2):
        @pl.when(core == side)
        def _():
            for p, r, base, rows in runs:
                slot = (p & 1) ^ near
                if p >> 1 == side:
                    own_ref[slot, base + r:base + r + 8, :] = rows
                else:
                    send_ref[slot, base + r:base + r + 8, :] = rows.astype(LOW)


def backward_kernel(dims, d, lt, n_wait, *refs):
    n_ch, n_tok, rows, width, chans, inner, rank, states, taps = dims
    total = rows * n_ch
    length = total // 8
    xd = rank + 2 * states
    base = d * xd
    first = base + rank
    sl = tile(lt)
    last_tile = lt == chans // LANES - 1
    refs = list(refs)

    def take(n):
        out = refs[:n]
        del refs[:n]
        return out

    (gy_ref, act_ref, stp_ref, sgm_ref, picked_ref, gains_ref, bb_ref, cb_ref, a_ref, h_ref, dlog_ref, skip_ref,
     stepw_ref, er_ref) = take(14)
    before = take(2)
    take(n_wait)
    gpick_ref, = take(1)
    if last_tile:
        low_ref, = take(1)
    else:
        q_ref, = take(1)
    gact_ref, gstepw_ref, gdlog_ref, misc_ref = take(4)
    if last_tile:
        q_ref, = take(1)
    r2_ref, gu_ref, gs_ref, gpre_ref, stepw_pad_ref = refs

    rate = -jnp.exp(dlog_ref[d, :, sl])
    for n in range(states):
        r2_ref[n] = jnp.broadcast_to(rate[n:n + 1] * LOG2E, (8, LANES))
    zero = jnp.zeros((8, LANES), F32)

    def against(j):
        return pl.multiple_of((j if d else length - 1 - j) * 8, 8)

    def ends_back(j2, state):
        state = list(state)
        at = [against(2 * j2 + jj) for jj in range(2)]
        gy = [gy_ref[lt, pl.ds(r0, 8), :] for r0 in at]
        for n in range(states):
            for jj, r0 in enumerate(at):
                state[n] = a_ref[lt, pl.ds(r0, 8), lane(n)] * (cb_ref[pl.ds(r0, 8), lane(n)] * gy[jj] + state[n])
        return tuple(state)

    back = over_pairs(length, ends_back, (zero,) * states)
    begin = [link_blocks(gains_ref[lt, n], back[n], d == 1) for n in range(states)]

    def backward(j2, state):
        grad, rate_sum = list(state[:states]), list(state[states:])
        at = [against(2 * j2 + jj) for jj in range(2)]
        r16 = pl.multiple_of((2 * j2 if d else length - 2 - 2 * j2) * 8, 16)
        gy = [gy_ref[lt, pl.ds(r0, 8), :] for r0 in at]
        step = [stp_ref[lt, pl.ds(r0, 8), :] for r0 in at]
        u = [step[jj] * act_ref[lt, pl.ds(r0, 8), :] for jj, r0 in enumerate(at)]
        gu = [[None, None], [None, None]]
        gs = [[None, None], [None, None]]
        for n in range(states):
            prods = []
            for jj, r0 in enumerate(at):
                g = cb_ref[pl.ds(r0, 8), lane(n)] * gy[jj] + grad[n]
                prods.append(g * u[jj])
                term = g * bb_ref[pl.ds(r0, 8), lane(n)]
                gu[jj][n % 2] = term if gu[jj][n % 2] is None else gu[jj][n % 2] + term
                grad[n] = a_ref[lt, pl.ds(r0, 8), lane(n)] * g
                q = grad[n] * h_ref[lt, pl.ds(r0, 8), lane(n)]
                rate_sum[n] = rate_sum[n] + q * step[jj]
                term = q * r2_ref[n]
                gs[jj][n % 2] = term if gs[jj][n % 2] is None else gs[jj][n % 2] + term
            value = jnp.concatenate(prods if d else prods[::-1], axis=0).astype(LOW)
            if lt:
                value = value + before[1][pl.ds(r16, 16), lane(n)]
            q_ref[pl.ds(r16, 16), lane(n)] = value
        for jj, r0 in enumerate(at):
            gu_ref[pl.ds(r0, 8), :] = gu[jj][0] + gu[jj][1]
            gs_ref[pl.ds(r0, 8), :] = gs[jj][0] + gs[jj][1]
        return tuple(grad) + tuple(rate_sum)

    last = over_pairs(length, backward, tuple(begin) + (zero,) * states)
    for n in range(states):
        gdlog_ref[n:n + 1, :] = jnp.sum(last[states + n], axis=0, keepdims=True) * rate[n:n + 1]
    misc_ref[...] = jnp.zeros_like(misc_ref)

    def post_rows(r0):
        rr = pl.ds(r0, BLOCK)
        active = act_ref[lt, rr, :]
        gu = gu_ref[rr, :]
        gy = gy_ref[lt, rr, :]
        gpre = (gs_ref[rr, :] * LN2 + gu * active) * sgm_ref[lt, rr, :]
        gpre_ref[rr, :] = gpre
        gact_ref[rr, :] = gu * stp_ref[lt, rr, :] + skip_ref[d:d + 1, sl] * gy
        misc_ref[0:1, :] += jnp.sum(gpre, axis=0, keepdims=True)
        misc_ref[1:2, :] += jnp.sum(gy * active, axis=0, keepdims=True)

    over_rows(total, post_rows)
    stepw_pad_ref[...] = jnp.zeros_like(stepw_pad_ref)
    stepw_pad_ref[base:base + rank, :] = stepw_ref[d, :, sl]
    gpre = gpre_ref[...]
    gpick = mm3(mm_nt, gpre, stepw_pad_ref[...]) + before[0][...]
    if last_tile:
        gpick = gpick + pltpu.roll(mm(q_ref[...], er_ref[...]), first, 1)
        low_ref[...] = gpick.astype(LOW)
    gpick_ref[...] = gpick
    gstepw_ref[...] = mm3(mm_tn, picked_ref[d], gpre)[base:base + rank, :]


def conv_back(dims, d, pos_ref, rem_ref, gpick_refs, gact_refs, act_ref, dsil_ref, sigs_ref, pack_ref, gsig_ref,
              gsel_ref, gconv_ref, gcp_ref, ext_ref, gcs_ref):
    n_ch, n_tok, rows, width, chans, inner, rank, states, taps = dims
    total = rows * n_ch
    nt = chans // LANES
    halo = 8 * (taps - 1)
    xd = rank + 2 * states
    gpick = gpick_refs[0][...]
    for k in range(1, n_ch):
        gpick = gpick + gpick_refs[k][...].astype(F32)
    spot = lax.broadcasted_iota(jnp.int32, (total, LANES), 1)
    gpick = jnp.where((spot >= d * xd) & (spot < (d + 1) * xd), gpick, 0.0)
    high, low = split(gpick)
    sel = pack_ref[0:LANES, :]
    gcp_ref[pl.ds(halo, total), :] = mm(high, sel) + mm(low, sel)
    gsel_ref[...] = mm3(mm_tn, gpick, wide(act_ref))[d * xd:(d + 1) * xd, :]
    ext_ref[pl.ds(halo, total), :] = sigs_ref[0].astype(F32)
    halo_fill(ext_ref, total, halo, slice(None))
    gcs_ref[...] = jnp.zeros_like(gcs_ref)
    conv = conv_rows_of(pack_ref, taps)

    def fold8(x):
        out = x[0:8]
        for i in range(8, BLOCK, 8):
            out = out + x[i:i + 8]
        return out

    def conv_rows(r0):
        rr = pl.ds(r0, BLOCK)
        inside = rem_ref[rr, :] if d else pos_ref[rr, :]
        for lt in range(nt):
            sl = tile(lt)
            gc = (gcp_ref[pl.ds(r0 + halo, BLOCK), sl] + gact_refs[lt][rr, :]) * dsil_ref[lt, rr, :]
            gcp_ref[pl.ds(r0 + halo, BLOCK), sl] = gc
            gcs_ref[taps, :, sl] += fold8(gc)
            gcs_ref[taps - 1, :, sl] += fold8(gc * ext_ref[pl.ds(r0 + halo, BLOCK), sl])
            for lag in range(1, taps):
                far = ext_ref[pl.ds(r0 + (halo + 8 * lag if d else halo - 8 * lag), BLOCK), sl]
                gcs_ref[taps - 1 - lag, :, sl] += fold8(jnp.where(inside >= lag, gc * far, 0.0))

    over_rows(total, conv_rows)
    halo_fill(gcp_ref, total, halo, slice(None))

    def signal_rows(r0):
        rr = pl.ds(r0, BLOCK)
        inside = pos_ref[rr, :] if d else rem_ref[rr, :]
        for lt in range(nt):
            sl = tile(lt)
            at = d * (taps + 1)
            summed = conv[at + taps - 1:at + taps, sl] * gcp_ref[pl.ds(r0 + halo, BLOCK), sl]
            for lag in range(1, taps):
                far = gcp_ref[pl.ds(r0 + (halo - 8 * lag if d else halo + 8 * lag), BLOCK), sl]
                summed = summed + conv[at + taps - 1 - lag:at + taps - lag, sl] * jnp.where(inside >= lag, far, 0.0)
            gsig_ref[rr, sl] = summed

    over_rows(total, signal_rows)
    gconv_ref[...] = jnp.zeros_like(gconv_ref)
    for k in range(taps + 1):
        gconv_ref[k:k + 1, :] = jnp.sum(gcs_ref[k], axis=0, keepdims=True)


def first_conv_kernel(dims, n_wait, pos_ref, rem_ref, *refs):
    n_ch, nt = dims[0], dims[4] // LANES
    gpicks, gacts, refs = refs[:n_ch], refs[n_ch:n_ch + nt], refs[n_ch + nt:]
    conv_back(dims, 0, pos_ref, rem_ref, gpicks, gacts, *refs[:4], *refs[4 + n_wait:])


def second_conv_kernel(dims, pos_ref, rem_ref, *refs):
    n_ch, n_tok, rows, width, chans, inner, rank, states, taps = dims
    nt = chans // LANES
    refs = list(refs)

    def take(n):
        out = refs[:n]
        del refs[:n]
        return out

    gpicks, gacts, rest, _ = take(n_ch), take(nt), take(4), take(2)
    gsig0_ref, gsel0_ref, gconv0_ref, normed_ref, ggate_ref, xp_ref, win_ref = take(7)
    tiles = [[take(3) for _ in range(nt)] for _ in range(2)]
    (gsig_ref, own_ref, send_ref, gcp_ref, ext_ref, gcs_ref, gsum_ref, gsel_ref, gconv_ref, small_ref, gain_ref) = refs
    conv_back(dims, 1, pos_ref, rem_ref, gpicks, gacts, *rest, gsum_ref, gsel_ref, gconv_ref, gcp_ref, ext_ref,
              gcs_ref)
    me = lax.axis_index("ch")
    gsig = (gsum_ref[...] + gsig0_ref[...]).astype(LOW)
    gsig_ref[...] = gsig
    gn = grad_normed(dims, me, gsig, ggate_ref, win_ref)
    xp = xp_ref[...].astype(F32)
    scale = lax.rsqrt(jnp.mean(xp * xp, axis=1, keepdims=True) + norm_eps)
    ggain = jnp.sum(gn * xp * scale, axis=0, keepdims=True)
    gin = mm_tn(normed_ref[...], gsig)
    places = small_places(dims)
    small_ref[...] = jnp.zeros_like(small_ref)
    xd = rank + 2 * states
    for d in range(2):
        at = places["select"] + d * xd
        small_ref[at:at + xd, :] = (gsel0_ref, gsel_ref)[d][...]
        conv_ref = (gconv0_ref, gconv_ref)[d]
        at = places["taps"] + d * taps
        small_ref[at:at + taps, :] = conv_ref[0:taps, :]
        small_ref[places["bias"] + d:places["bias"] + d + 1, :] = conv_ref[taps:taps + 1, :]
        for lt in range(nt):
            gstepw_ref, gdlog_ref, misc_ref = tiles[d][lt]
            sl = tile(lt)
            at = places["step"] + d * rank
            small_ref[at:at + rank, sl] = gstepw_ref[...]
            at = places["decay"] + d * states
            small_ref[at:at + states, sl] = gdlog_ref[...]
            small_ref[places["sbias"] + d:places["sbias"] + d + 1, sl] = misc_ref[0:1, :]
            small_ref[places["skip"] + d:places["skip"] + d + 1, sl] = misc_ref[1:2, :]
    gain_ref[...] = jnp.zeros_like(gain_ref)
    for i in range(width // chans):
        gain_ref[i:i + 1, :] = ggain[:, i * chans:(i + 1) * chans]
    pack(own_ref, send_ref, [[gin], [gain_ref[...]], [small_ref[...]]])


def grad_normed(dims, me, gsig, ggate_ref, win_ref):
    n_ch, n_tok, rows, width, chans, inner, rank, states, taps = dims
    return mm_nt(gsig, win_ref[:, pl.ds(pl.multiple_of(me * chans, LANES), chans)]) + mm_nt(
        ggate_ref[...], win_ref[:, pl.ds(pl.multiple_of(inner + me * chans, LANES), chans)]
    )


def normed_kernel(dims, gsig_ref, ggate_ref, win_ref, *refs):
    n_ch, n_tok, rows, width, chans, inner, rank, states, taps = dims
    blk_refs, gn_own_ref, part_refs = refs[:n_ch - 1], refs[n_ch - 1], refs[n_ch:]
    me = lax.axis_index("ch")
    gn = grad_normed(dims, me, gsig_ref[...], ggate_ref, win_ref)
    token_rows(me, gn, n_ch, rows, rows * n_ch, gn_own_ref, [ref.at[rows:2 * rows] for ref in part_refs])
    for blk_ref, part_ref in zip(blk_refs, part_refs):
        part_ref[0:rows, :] = blk_ref[...]


def small_places(dims):
    n_ch, n_tok, rows, width, chans, inner, rank, states, taps = dims
    places, at = {}, 0
    for name, size in (
        ("select", 2 * (rank + 2 * states)), ("step", 2 * rank), ("decay", 2 * states), ("taps", 2 * taps),
        ("bias", 2), ("sbias", 2), ("skip", 2),
    ):
        places[name] = at
        at += size
    places["end"] = round_up(at, 8)
    return places


def token_kernel(n_ch, at, tok_ref, cot_ref, gain_ref, blk_ref, gn_ref, *refs):
    parts = refs[:n_ch - 1]
    out_ref, gtok_ref, mark_ref = refs[n_ch - 1:]
    mark_ref[...] = jnp.zeros_like(mark_ref)
    tokens = tok_ref[...].astype(F32)
    out = tokens + blk_ref[...]
    gn = gn_ref[...]
    rows = tok_ref.shape[0]
    for part in parts:
        out = out + part[at:at + rows, :].astype(F32)
        gn = gn + part[at + rows:at + 2 * rows, :].astype(F32)
    out_ref[...] = out.astype(LOW)
    scale = lax.rsqrt(jnp.mean(tokens * tokens, axis=1, keepdims=True) + norm_eps)
    unit = tokens * scale
    scaled = gn * gain_ref[...][None, :]
    gtok_ref[...] = cot_ref[...].astype(F32) + scale * (
        scaled - unit * jnp.mean(scaled * unit, axis=1, keepdims=True)
    )


def join_kernel(n_ch, rb, base_ref, *refs):
    others, out_ref = refs[:n_ch - 1], refs[-1]
    out_ref[0:rb, :] = base_ref[0:rb, :]
    mixed = base_ref[rb:rb + 16, :].astype(F32)
    gain = mixed[0:8]
    for c, other in enumerate(others):
        out_ref[(c + 1) * rb:(c + 2) * rb, :] = other[0:rb, :]
        gain = gain + other[rb:rb + 16, :].astype(F32)[0:8]
    at = n_ch * rb
    out_ref[at:at + 16, :] = jnp.concatenate([gain, mixed[8:16]], axis=0).astype(LOW)
    out_ref[at + 16:, :] = base_ref[rb + 16:, :]


def my_pieces():
    core, near = my_place()
    return [(core ^ (k >> 1)) * 2 + (near ^ (k & 1)) for k in range(PIECES)]


def place_columns(dims, every, at, block_ref, gin_hbm, first, sems):
    n_ch, n_tok, rows, width, chans, inner, rank, states, taps = dims
    rb = chunk_rows(PIECES, width)
    me = lax.axis_index("ch")
    copies = []
    for k, piece in enumerate(my_pieces()):
        rr = pl.ds(pl.multiple_of(piece * rb, 8), rb)
        for c in range(n_ch):
            j = lax.rem(me + c, n_ch) * chans
            block_ref[k, :, pl.ds(pl.multiple_of(j, LANES), chans)] = every[k][
                at + c * rb:at + (c + 1) * rb, :
            ].astype(F32)
        copies.append(pltpu.make_async_copy(block_ref.at[k], gin_hbm.at[rr, first:first + inner], sems.at[k]))
        copies[-1].start()
    return copies


def early_result_kernel(dims, every_ref, gin_hbm, gout_hbm, mark_ref, block_ref, gout_ref, sems):
    n_ch, n_tok, rows, width, chans, inner, rank, states, taps = dims
    ra = chunk_rows(PIECES, chans)
    copies = place_columns(dims, [every_ref.at[k] for k in range(PIECES)], ra, block_ref, gin_hbm, inner, sems)
    for k, piece in enumerate(my_pieces()):
        gout_ref[pl.ds(pl.multiple_of(piece * ra, 8), ra), :] = every_ref[k, 0:ra, :].astype(F32)
    mark_ref[...] = jnp.zeros_like(mark_ref)
    copies.append(pltpu.make_async_copy(gout_ref, gout_hbm, sems.at[PIECES]))
    copies[-1].start()
    for copy in copies:
        copy.wait()


def late_result_kernel(dims, *refs):
    every, gin_hbm, refs = refs[:PIECES], refs[PIECES + 1], refs[PIECES + 2:]
    n_ch, n_tok, rows, width, chans, inner, rank, states, taps = dims
    outs, stages, (small_ref, block_ref, sems) = refs[:8], refs[8:16], refs[16:]
    ggain_ref, gtaps_ref, gbias_ref, gsel_ref, gstep_ref, gsbias_ref, gdecay_ref, gskip_ref = stages
    places = small_places(dims)
    rb, rs = chunk_rows(PIECES, width), chunk_rows(PIECES, places["end"])
    at = n_ch * rb
    gain = 0.0
    for k, piece in enumerate(my_pieces()):
        mixed = every[k][at:at + 8 + rs, :].astype(F32)
        small_ref[pl.ds(pl.multiple_of(piece * rs, 8), rs), :] = mixed[8:]
        gain = gain + mixed[0:8]
    ggain_ref[...] = gain[0]
    xd = rank + 2 * states
    for d in range(2):
        for ref, name, size in ((gsel_ref, "select", xd), (gstep_ref, "step", rank), (gdecay_ref, "decay", states),
                                (gtaps_ref, "taps", taps)):
            first = places[name] + d * size
            ref[d] = small_ref[first:first + size, :]
    for ref, name in ((gbias_ref, "bias"), (gsbias_ref, "sbias"), (gskip_ref, "skip")):
        ref[...] = small_ref[places[name]:places[name] + 2, :]
    copies = [pltpu.make_async_copy(a, b, sems.at[PIECES + i]) for i, (a, b) in enumerate(zip(stages, outs))]
    for copy in copies:
        copy.start()
    copies += place_columns(dims, every, 0, block_ref, gin_hbm, 0, sems)
    for copy in copies:
        copy.wait()


def chunk_rows(n_tok, total):
    return round_up(-(-total // n_tok), 8)


def vmem_specs(n):
    return [pl.BlockSpec(memory_space=pltpu.VMEM)] * n


def kernel_call(kernel, name, operands, outs, scratch, limit, us, places=(), hbm_outs=(), aliases=()):
    specs = vmem_specs(len(operands))
    for i, space in places:
        specs[i] = pl.BlockSpec(memory_space=space)
    return pl.pallas_call(
        kernel,
        name=name,
        out_shape=outs,
        in_specs=specs,
        out_specs=[pl.BlockSpec(memory_space=pl.ANY if i in hbm_outs else pltpu.VMEM) for i in range(len(outs))],
        scratch_shapes=scratch,
        input_output_aliases=dict(aliases),
        compiler_params=pltpu.CompilerParams(vmem_limit_bytes=limit * 1024 * 1024),
        cost_estimate=pl.CostEstimate(flops=int(us * 1e7), bytes_accessed=int(us * 3e4), transcendentals=0),
    )(*operands)


def rotated(x, n_ch):
    return [x] + [
        lax.ppermute(x, "ch", [((i + k) % n_ch, i) for i in range(n_ch)]) for k in range(1, n_ch)
    ]


def sent(parts, n_ch):
    return [
        lax.ppermute(parts[k - 1], "ch", [(i, (i + k) % n_ch) for i in range(n_ch)]) for k in range(1, n_ch)
    ]


def partner_pairs(n_tok, stride):
    return [(i, i ^ stride) for i in range(n_tok)]


def swap(x, n_tok, stride):
    return lax.ppermute(x, "tok", partner_pairs(n_tok, stride))


def near_strides():
    return [1, 2]


def far_strides(n_tok):
    strides, s = [], 4
    while s < n_tok:
        strides.append(s)
        s *= 2
    return strides


def add_kernel(halving, last, own_ref, got_ref, *refs):
    send_ref = refs[-1]
    if halving:
        refs[-2][...] = own_ref[0] + got_ref[0].astype(F32)
        send_ref[...] = (own_ref[1] + got_ref[1].astype(F32)).astype(LOW)
    else:
        both = own_ref[...] + got_ref[...].astype(F32)
        send_ref[...] = both.astype(LOW)
        if not last:
            refs[-2][...] = both


class Reduction:
    def __init__(self, own, send, n_tok, limit):
        self.own, self.n_tok, self.limit = own, n_tok, limit
        self.strides = [2] + far_strides(n_tok)
        self.got = swap(send, n_tok, 1)

    def done(self):
        return self.own.dtype == LOW

    def add(self, *wait):
        halving, last = self.own.ndim == 3, not self.strides
        shape = self.own.shape[-2:]
        outs = kernel_call(
            functools.partial(add_kernel, halving, last), "add_kernel", (self.own, self.got, *wait),
            ([] if last else [jax.ShapeDtypeStruct(shape, F32)]) + [jax.ShapeDtypeStruct(shape, LOW)], [], self.limit,
            0.1, [(i, pl.ANY) for i in range(2, 2 + len(wait))],
        )
        self.own = outs[0]
        if not last:
            self.got = swap(outs[1], self.n_tok, self.strides.pop(0))


def stack_kernel(spans, *refs):
    at = 0
    for (first, rows), ref in zip(spans, refs):
        refs[-1][at:at + rows, :] = ref[first:first + rows, :]
        at += rows


def stack(parts, wait, limit):
    parts = [part if isinstance(part, tuple) else (part, 0, part.shape[0]) for part in parts]
    arrays, spans = [part[0] for part in parts], [part[1:] for part in parts]
    shape = (sum(rows for _, rows in spans), arrays[0].shape[1])
    return kernel_call(
        functools.partial(stack_kernel, spans), "stack_kernel", (*arrays, wait), [jax.ShapeDtypeStruct(shape, LOW)], [],
        limit, 0.1, [(len(parts), pl.ANY)],
    )[0]


def local(
    tokens,
    cotangent,
    norm_gain,
    in_proj,
    conv_weight,
    conv_bias,
    select_proj,
    step_proj,
    step_bias,
    decay_log,
    skip_gain,
    out_proj,
    clip_lengths,
):
    n_ch, n_tok = lax.axis_size("ch"), lax.axis_size("tok")
    rows, width = tokens.shape
    real = conv_bias.shape[1]
    taps, rank, states = conv_weight.shape[1], step_proj.shape[1], decay_log.shape[1]
    chans = round_up(real, LANES)
    extra = chans - real
    xd = rank + 2 * states

    def pad_last(x):
        return jnp.pad(x, [(0, 0)] * (x.ndim - 1) + [(0, extra)]) if extra else x

    if extra:
        in_proj = pad_last(in_proj.reshape(width, 2 * n_ch, real)).reshape(width, 2 * n_ch * chans)
        step_proj, step_bias, decay_log, skip_gain = map(pad_last, (step_proj, step_bias, decay_log, skip_gain))
        out_proj = jnp.pad(out_proj, ((0, extra), (0, 0)))
    inner = n_ch * chans
    total = rows * n_ch
    nt = chans // LANES
    span = states * LANES
    halo = 8 * (taps - 1)
    fold = width // chans
    dims = (n_ch, n_tok, rows, width, chans, inner, rank, states, taps)
    limit = 16 if total <= 256 else 60
    shape = jax.ShapeDtypeStruct
    vm = pltpu.VMEM
    one = (nt, total, LANES)
    dma = pltpu.SemaphoreType.DMA
    spot = shape((total, LANES), jnp.int32)

    def far(*arrays):
        return [pltpu.with_memory_space_constraint(x, pltpu.HBM) for x in arrays]

    tok_parts = rotated(tokens, n_ch)
    (packed,) = kernel_call(
        functools.partial(weight_kernel, dims), "weight_kernel",
        far(select_proj.transpose(0, 2, 1), conv_weight, conv_bias), [shape((LANES + 32, chans), LOW)],
        [vm((2, xd, real), F32), vm((2, taps, real), F32), vm((2, real), F32), dma((3,))], limit, 20,
        [(i, pltpu.HBM) for i in range(3)],
    )
    pack_parts = rotated(packed, n_ch)
    fetched = (in_proj, tokens, norm_gain, cotangent)
    win, own, gain, cot_own = kernel_call(
        functools.partial(fetch_kernel, len(fetched)), "fetch_kernel", (*far(*fetched), packed),
        [shape(x.shape, x.dtype) for x in fetched], [dma((FETCHES + len(fetched) - 1,))], limit, 20,
        [(i, pltpu.HBM) for i in range(len(fetched))] + [(len(fetched), pl.ANY)],
    )
    normed, xp, sigs, gate, pos, rem = kernel_call(
        functools.partial(norm_kernel, dims), "norm_kernel",
        (*far(clip_lengths), own, gain, win, *tok_parts[1:]),
        [shape((total, width), LOW), shape((total, width), LOW), shape((n_ch, total, chans), LOW),
         shape((total, chans), LOW), spot, spot],
        [pltpu.SMEM(clip_lengths.shape, jnp.int32), dma], limit, 50, [(0, pltpu.HBM)],
    )
    cot_parts = rotated(cot_own, n_ch)
    ext = vm((total + 2 * halo, chans), F32)
    act0, act1, dsil0, dsil1, part = kernel_call(
        functools.partial(own_front_kernel, dims), "own_front_kernel", (packed, sigs, pos, rem),
        [shape(one, F32)] * 4 + [shape((2, total, LANES), F32)], [ext], limit, 1,
    )
    picked, stp0, stp1, sgm0, sgm1 = kernel_call(
        functools.partial(front_kernel, dims), "front_kernel",
        (*pack_parts[1:], sigs, pos, rem, part, *far(step_proj, step_bias)),
        [shape((2, total, LANES), F32)] + [shape(one, F32)] * 4,
        [ext, vm((2, LANES, chans), F32), vm((total, chans), F32), vm(one, F32), vm(one, F32),
         vm((2, rank, chans), F32), vm((2, chans), F32), dma((2,))],
        limit, 1, ((n_ch + 3, pltpu.HBM), (n_ch + 4, pltpu.HBM)),
    )

    ra, rb = chunk_rows(PIECES, chans * fold), chunk_rows(PIECES, width)
    r1 = ra + rb
    cotp, gg, gy = kernel_call(
        functools.partial(gate_kernel, dims), "gate_kernel", (*cot_parts, out_proj, gate, picked),
        [shape((total, width), LOW), shape((total, chans), LOW), shape(one, F32)], [], limit, 1,
        [(n_ch + 2, pl.ANY)],
    )
    spread, gather = selectors(states)
    scans = []
    for d, (act, stp) in enumerate(((act0, stp0), (act1, stp1))):
        scans.append(kernel_call(
            functools.partial(forward_kernel, dims, d), "forward_kernel_%d" % d,
            (gy, act, stp, picked, decay_log, rem if d else pos, spread, gather),
            [shape(one, F32), shape((nt, states, 8, LANES), F32)] + [shape((total, span), F32)] * 2
            + [shape((nt, total, span), F32)] * 2 + [shape((total, LANES), F32)],
            [vm((nt, states, 8, LANES), F32), vm((total, LANES), LOW), vm((total, span), LOW)],
            limit, 1,
        ))
    outs = kernel_call(
        functools.partial(out_kernel, dims), "out_kernel",
        (scans[0][0], scans[1][0], act0, act1, skip_gain, gate, gg, normed, cotp),
        [shape((total, chans), LOW), shape((total, chans), LOW), shape((2, r1, chans), F32),
         shape((2, r1, chans), LOW)],
        [], limit, 1,
    )
    gated, ggate, own1, send1 = outs

    early = Reduction(own1, send1, n_tok, limit)
    gpick_parts, gacts, tile_outs = [], [], [[], []]
    for d, (act, stp, sgm) in enumerate(((act0, stp0, sgm0), (act1, stp1, sgm1))):
        gains, bb, cb, decays, before_states, gmap = scans[d][1:]
        before = (gmap, gmap)
        gacts.append([])
        for lt in range(nt):
            final = lt == nt - 1
            operands = (gy, act, stp, sgm, picked, gains, bb, cb, decays, before_states, decay_log, skip_gain,
                        step_proj, gather, *before)
            wait = [early.own] if (d, lt) in ((1, 0), (1, nt - 1)) else []
            outs = kernel_call(
                functools.partial(backward_kernel, dims, d, lt, len(wait)), "backward_kernel_%d%d" % (d, lt),
                (*operands, *wait),
                [shape((total, LANES), F32)]
                + ([shape((total, LANES), LOW)] if final else [shape((total, span), LOW)])
                + [shape((total, LANES), F32), shape((rank, LANES), F32), shape((states, LANES), F32),
                   shape((8, LANES), F32)],
                ([vm((total, span), LOW)] if final else [])
                + [vm((states, 8, LANES), F32), vm((total, LANES), F32), vm((total, LANES), F32),
                   vm((total, LANES), F32), vm((LANES, LANES), F32)],
                limit, 0.5, [(len(operands) + i, pl.ANY) for i in range(len(wait))],
            )
            before = tuple(outs[:2])
            gacts[d].append(outs[2])
            tile_outs[d].extend(outs[-3:])
            if early.strides and (d, lt) in ((0, 0), (0, nt - 1), (1, nt - 2)):
                early.add(outs[-1])
        gpick_parts.append([outs[0]] + rotated(outs[1], n_ch)[1:])

    wait = [tile_outs[1][-1]]
    conv_scratch = [vm((total + 2 * halo, chans), F32), vm((total + 2 * halo, chans), F32),
                    vm((taps + 1, 8, chans), F32)]
    operands = (pos, rem, *gpick_parts[0], *gacts[0], act0, dsil0, sigs, packed, *wait)
    gsig0, gsel0, gconv0 = kernel_call(
        functools.partial(first_conv_kernel, dims, len(wait)), "first_conv_kernel", operands,
        [shape((total, chans), F32), shape((xd, chans), F32), shape((8, chans), F32)],
        conv_scratch, limit, 0.5, [(i, pl.ANY) for i in range(len(operands) - len(wait), len(operands))],
    )
    outs = kernel_call(
        functools.partial(block_kernel, dims), "block_kernel", (gated, out_proj, gconv0),
        [shape((rows, width), F32)] + [shape((rows, width), LOW)] * (n_ch - 1), [], limit, 0.5, [(2, pl.ANY)],
    )
    blk_own, blk_parts = outs[0], outs[1:]
    places = small_places(dims)
    rs = chunk_rows(PIECES, places["end"])
    r2 = rs + rb + 8
    gsig, own2, send2 = kernel_call(
        functools.partial(second_conv_kernel, dims), "second_conv_kernel",
        (pos, rem, *gpick_parts[1], *gacts[1], act1, dsil1, sigs, packed, blk_own, early.got, gsig0, gsel0, gconv0, normed, ggate, xp,
         win, *tile_outs[0], *tile_outs[1]),
        [shape((total, chans), LOW), shape((2, r2, chans), F32), shape((2, r2, chans), LOW)],
        conv_scratch + [vm((total, chans), F32), vm((xd, chans), F32), vm((8, chans), F32),
                        vm((places["end"], chans), F32), vm((8, chans), F32)],
        limit, 0.5, [(6 + n_ch + nt, pl.ANY), (7 + n_ch + nt, pl.ANY)],
    )
    outs = kernel_call(
        functools.partial(normed_kernel, dims), "normed_kernel", (gsig, ggate, win, *blk_parts),
        [shape((rows, width), F32)] + [shape((2 * rows, width), LOW)] * (n_ch - 1), [], limit, 0.5,
    )
    gn_own, token_parts = outs[0], outs[1:n_ch]

    late = Reduction(own2, send2, n_tok, limit)
    early.add(gn_own)
    while not early.done():
        early.add()
    gate = (early.own, ra, rb)
    if n_ch == 2 and width == chans:
        token_got = gates = sent([stack([gate, token_parts[0]], gn_own, limit)], n_ch)
    else:
        token_got, gates = sent(token_parts, n_ch), rotated(early.own[ra:], n_ch)[1:]
    late.add(gn_own)
    late.add()
    block_out, grad_tokens, mark = kernel_call(
        functools.partial(token_kernel, n_ch, token_got[0].shape[0] - 2 * rows), "token_kernel",
        (own, cot_own, gain, blk_own, gn_own, *token_got),
        [shape((rows, width), LOW), shape((rows, width), F32), shape((8, LANES), F32)], [], limit, 0.5,
    )
    early_piece = stack([early.own, *((got, 0, rb) for got in gates)], mark, limit)
    first_got = swap(early_piece, n_tok, 2)
    late.add(mark)
    while not late.done():
        late.add()
    early_pair = stack([early_piece, first_got], late.own, limit).reshape(2, ra + n_ch * rb, chans)
    every1 = jnp.concatenate([early_pair, swap(early_pair, n_tok, 1)], axis=0)
    assert rb % 16 == 0 and (rs + 8) % 16 == 0
    shared = late.own[:rb + 16]
    sides = [[], []]
    for side in range(2):
        for c in range(n_ch):
            if (side, c) == (0, 0):
                sides[0].append(late.own)
                continue
            pairs = [
                ((i ^ (2 * side)) * n_ch + (j + c) % n_ch, i * n_ch + j) for i in range(n_tok) for j in range(n_ch)
            ]
            sides[side].append(lax.ppermute(shared if c else late.own, ("tok", "ch"), pairs))

    def join(wait):
        mine = [
            kernel_call(
                functools.partial(join_kernel, n_ch, rb), "join_kernel", (*parts, wait),
                [shape((n_ch * rb + 8 + rs, chans), LOW)], [], limit, 0.5, [(n_ch, pl.ANY)],
            )[0] for parts in sides
        ]
        return mine + [swap(piece, n_tok, 1) for piece in mine]

    if not extra and fold == 1 and ra * PIECES == chans and rb * PIECES == width:
        block = vm((PIECES, rb, inner), F32)
        gin, gout, mark = kernel_call(
            functools.partial(early_result_kernel, dims), "early_result_kernel", (every1,),
            [shape((width, 2 * inner), F32), shape((chans, width), F32), shape((8, LANES), F32)],
            [block, vm((chans, width), F32), dma((PIECES + 1,))], limit, 2, hbm_outs=(0, 1),
        )
        every2 = join(mark)
        small_shapes = [(width,), (2, taps, chans), (2, chans), (2, xd, chans), (2, rank, chans), (2, chans),
                        (2, states, chans), (2, chans)]
        gin, ggain, gtaps, gbias, gsel, gstep, gsbias, gdecay, gskip = kernel_call(
            functools.partial(late_result_kernel, dims), "late_result_kernel",
            (*every2, gin),
            [shape((width, 2 * inner), F32)] + [shape(x, F32) for x in small_shapes],
            [vm(x, F32) for x in small_shapes] + [vm((rs * PIECES, chans), F32), block, dma((PIECES + 8,))], limit, 2,
            [(PIECES, pl.ANY)], hbm_outs=range(9), aliases={PIECES: 0},
        )
    else:
        every2 = jnp.stack(join(late.own))
        me, tok = lax.axis_index("ch"), lax.axis_index("tok")
        mine = (tok & 1) * 2 + ((tok >> 1) & 1)
        at = jnp.arange(PIECES) ^ mine
        every1, every2 = every1[at], every2[at]
        turn = (jnp.arange(n_ch) - me) % n_ch
        gate = every1[:, ra:].reshape(PIECES, n_ch, rb, chans)
        signal = every2[:, :n_ch * rb].reshape(PIECES, n_ch, rb, chans)
        gin = jnp.concatenate([signal[:, turn], gate[:, turn]], axis=1).transpose(0, 2, 1, 3)[..., :real]
        gin = gin.reshape(PIECES * rb, 2 * n_ch * real)[:width].astype(F32)
        gout = every1[:, :ra].reshape(PIECES * ra, chans)[:chans * fold]
        gout = jnp.concatenate([gout[i * chans:(i + 1) * chans] for i in range(fold)], axis=1)[:real].astype(F32)
        small = every2[:, n_ch * rb + 8:].reshape(PIECES * rs, chans).astype(F32)
        ggain = jnp.sum(every2[:, n_ch * rb:n_ch * rb + 8].astype(F32), axis=0)[:fold].reshape(width)

        def rows_of(name, size):
            return small[places[name]:places[name] + size]

        gsel, gstep, gdecay, gtaps = (
            rows_of(name, 2 * size).reshape(2, size, chans)[..., :real]
            for name, size in (("select", xd), ("step", rank), ("decay", states), ("taps", taps))
        )
        gbias, gsbias, gskip = (rows_of(name, 2)[:, :real] for name in ("bias", "sbias", "skip"))
    return (
        block_out,
        grad_tokens,
        ggain,
        gin,
        gtaps,
        gbias,
        gsel.transpose(0, 2, 1),
        gstep,
        gsbias,
        gdecay,
        gskip,
        gout,
    )


def solution(mesh):
    return jax.shard_map(
        local,
        mesh=mesh,
        in_specs=(
            P(("tok", "ch"), None),
            P(("tok", "ch"), None),
            P(),
            P(),
            P(None, None, "ch"),
            P(None, "ch"),
            P(None, "ch", None),
            P(None, None, "ch"),
            P(None, "ch"),
            P(None, None, "ch"),
            P(None, "ch"),
            P("ch", None),
            P("tok", None),
        ),
        out_specs=(
            P(("tok", "ch"), None),
            P(("tok", "ch"), None),
            P(),
            P(),
            P(None, None, "ch"),
            P(None, "ch"),
            P(None, "ch", None),
            P(None, None, "ch"),
            P(None, "ch"),
            P(None, None, "ch"),
            P(None, "ch"),
            P("ch", None),
        ),
        check_vma=False,
    )
```

```python
import functools
import math

import jax
import jax.numpy as jnp
import numpy as np
from jax import lax
from jax.experimental import pallas as pl
from jax.experimental.pallas import tpu as pltpu
from jax.sharding import PartitionSpec as P

norm_eps = 1e-05
F32 = jnp.float32
LOW = jnp.bfloat16
LANES = 128
HUGE_STEP = 1e30
LOG2E = math.log2(math.e)
LN2 = math.log(2.0)
BLOCK = 128
PAIRS = 8
PIECES = 4


def mm(a, b):
    return lax.dot_general(a, b, (((1,), (0,)), ((), ())), preferred_element_type=F32)


def mm_nt(a, b):
    return lax.dot_general(a, b, (((1,), (1,)), ((), ())), preferred_element_type=F32)


def mm_tn(a, b):
    return lax.dot_general(a, b, (((0,), (0,)), ((), ())), preferred_element_type=F32)


def split(x):
    high = x.astype(LOW)
    return high, (x - high.astype(F32)).astype(LOW)


def mm3(dot, a, b):
    a_high, a_low = split(a)
    b_high, b_low = split(b)
    return dot(a_high, b_high) + (dot(a_high, b_low) + dot(a_low, b_high))


def round_up(x, m):
    return -(-x // m) * m


def wide(ref, *lead):
    parts = [ref[lead + (i,)] for i in range(ref.shape[len(lead)])]
    return parts[0] if len(parts) == 1 else jnp.concatenate(parts, axis=-1)


def row_time(r, length):
    return (r & 7) * length + (r >> 3)


def clip_places(len_ref, total, shape):
    t = row_time(lax.broadcasted_iota(jnp.int32, shape, 0), total // 8)
    clips = len_ref.shape[1]
    ends = []
    acc = 0
    for c in range(clips):
        acc = acc + len_ref[0, c]
        ends.append(acc)
    start = jnp.zeros(shape, jnp.int32)
    end = jnp.full(shape, total, jnp.int32)
    for c in range(clips - 1):
        start = jnp.where(t >= ends[c], ends[c], start)
    for c in range(clips - 2, -1, -1):
        end = jnp.where(t < ends[c], ends[c], end)
    return t - start, end - 1 - t


def order_matrix(first, rows, first_token, tokens, total):
    r = lax.broadcasted_iota(jnp.int32, (rows, tokens), 0) + first
    t = lax.broadcasted_iota(jnp.int32, (rows, tokens), 1) + first_token
    return jnp.where(row_time(r, total // 8) == t, 1.0, 0.0).astype(LOW)


def take_tokens(first, rows, total):
    t = lax.broadcasted_iota(jnp.int32, (rows, total), 0) + first
    r = lax.broadcasted_iota(jnp.int32, (rows, total), 1)
    return jnp.where(row_time(r, total // 8) == t, 1.0, 0.0).astype(LOW)


def halo_fill(ext_ref, total, halo, sl):
    for q in range(halo // 8):
        tail = ext_ref[pl.ds(total + 8 * q, 8), sl]
        ext_ref[pl.ds(8 * q, 8), sl] = pltpu.roll(tail, 1, 0)
        head = ext_ref[pl.ds(halo + 8 * q, 8), sl]
        ext_ref[pl.ds(halo + total + 8 * q, 8), sl] = pltpu.roll(head, 7, 0)


def link_blocks(gain, added, toward_end):
    row = lax.broadcasted_iota(jnp.int32, gain.shape, 0)
    for k in (1, 2, 4):
        shift = k if toward_end else 8 - k
        inside = (row >= k) if toward_end else (row < 8 - k)
        added_near = jnp.where(inside, pltpu.roll(added, shift, 0), 0.0)
        gain_near = jnp.where(inside, pltpu.roll(gain, shift, 0), 1.0)
        added = added + gain * added_near
        gain = gain * gain_near
    if toward_end:
        return jnp.where(row >= 1, pltpu.roll(added, 1, 0), 0.0)
    return jnp.where(row < 7, pltpu.roll(added, 7, 0), 0.0)


def over_rows(total, body):
    def step(i, carry):
        body(pl.multiple_of(i * BLOCK, BLOCK))
        return carry

    lax.fori_loop(0, total // BLOCK, step, 0)


def over_pairs(length, body, init):
    def trip(i, carry):
        for q in range(PAIRS):
            carry = body(i * PAIRS + q, carry)
        return carry

    return lax.fori_loop(0, length // 2 // PAIRS, trip, init)


def tile(lt):
    return slice(lt * LANES, (lt + 1) * LANES)


def lane(n):
    return slice(n * LANES, (n + 1) * LANES)


def sigmoid(x):
    return 0.5 * jnp.tanh(0.5 * x) + 0.5


def fetch_all(sources, targets, sems):
    copies = [pltpu.make_async_copy(a, b, sems.at[i]) for i, (a, b) in enumerate(zip(sources, targets))]
    for copy in copies:
        copy.start()
    return copies


def weight_kernel(dims, select_hbm, taps_hbm, bias_hbm, packed_ref, select_ref, taps_ref, bias_ref, sems):
    taps, real = taps_ref.shape[1:]
    xd = select_ref.shape[1]
    for copy in fetch_all((select_hbm, taps_hbm, bias_hbm), (select_ref, taps_ref, bias_ref), sems):
        copy.wait()
    parts = [select_ref[0], select_ref[1], jnp.zeros((LANES - 2 * xd, real), F32)]
    packed_ref[0:LANES, 0:real] = jnp.concatenate(parts, axis=0).astype(LOW)
    parts = []
    for d in range(2):
        parts += [taps_ref[d], bias_ref[d:d + 1, :]]
    parts.append(jnp.zeros((16 - 2 * (taps + 1), real), F32))
    high, low = split(jnp.concatenate(parts, axis=0))
    packed_ref[LANES:LANES + 16, 0:real] = high
    packed_ref[LANES + 16:LANES + 32, 0:real] = low
    if real < packed_ref.shape[1]:
        packed_ref[:, real:] = jnp.zeros((LANES + 32, packed_ref.shape[1] - real), LOW)


def fetch_kernel(inner, chans, win_hbm, own_hbm, gain_hbm, cot_hbm, _, win_ref, own_ref, gain_ref, cot_ref, sems):
    first = pl.multiple_of(inner + lax.axis_index("ch") * chans, LANES)
    for copy in fetch_all(
        (win_hbm.at[:, 0:inner], win_hbm.at[:, pl.ds(first, chans)], own_hbm, gain_hbm, cot_hbm),
        (win_ref.at[:, 0:inner], win_ref.at[:, inner:inner + chans], own_ref, gain_ref, cot_ref), sems,
    ):
        copy.wait()


def norm_kernel(dims, len_hbm, own_ref, gain_ref, win_ref, *refs):
    n_ch, n_tok, rows, width, chans, inner, rank, states, taps = dims
    total = rows * n_ch
    toks = [own_ref, *refs[:n_ch - 1]]
    normed_ref, xp_ref, sigs_ref, gate_ref, pos_ref, rem_ref, len_ref, sem = refs[n_ch - 1:]
    me = lax.axis_index("ch")
    fetch = pltpu.make_async_copy(len_hbm, len_ref, sem)
    fetch.start()
    gain = gain_ref[...][None, :]
    for r0 in range(0, total, 256):
        rr = slice(r0, r0 + 256)
        xp = 0.0
        for k in range(n_ch):
            xp = xp + mm(order_matrix(r0, 256, lax.rem(me + k, n_ch) * rows, rows, total), toks[k][...])
        xp_ref[rr, :] = xp.astype(LOW)
        scale = lax.rsqrt(jnp.mean(xp * xp, axis=1, keepdims=True) + norm_eps)
        normed_ref[rr, :] = (xp * scale * gain).astype(LOW)
    normed = normed_ref[...]
    for k in range(n_ch):
        j = lax.rem(me + k, n_ch)
        sigs_ref[k] = mm(normed, win_ref[:, pl.ds(pl.multiple_of(j * chans, LANES), chans)]).astype(LOW)
    gate_ref[...] = mm(
        normed, win_ref[:, inner:inner + chans]
    ).astype(LOW)
    fetch.wait()
    pos, rem = clip_places(len_ref, total, (total, LANES))
    pos_ref[...] = pos
    rem_ref[...] = rem


def conv_silu(dims, k, sigs_ref, pack_ref, pos_ref, rem_ref, act_refs, dsil_refs, ext_ref):
    n_ch, n_tok, rows, width, chans, inner, rank, states, taps = dims
    total = rows * n_ch
    halo = 8 * (taps - 1)
    ext_ref[pl.ds(halo, total), :] = sigs_ref[k].astype(F32)
    halo_fill(ext_ref, total, halo, slice(None))
    conv = conv_rows_of(pack_ref, taps)

    def conv_rows(r0):
        pos_b = pos_ref[pl.ds(r0, BLOCK), :]
        rem_b = rem_ref[pl.ds(r0, BLOCK), :]
        for lt in range(chans // LANES):
            sl = tile(lt)
            for d in range(2):
                inside = rem_b if d else pos_b
                at = d * (taps + 1)
                summed = conv[at + taps:at + taps + 1, sl] + conv[at + taps - 1:at + taps, sl] * ext_ref[
                    pl.ds(r0 + halo, BLOCK), sl
                ]
                for lag in range(1, taps):
                    far = ext_ref[pl.ds(r0 + (halo + 8 * lag if d else halo - 8 * lag), BLOCK), sl]
                    summed = summed + conv[at + taps - 1 - lag:at + taps - lag, sl] * jnp.where(
                        inside >= lag, far, 0.0
                    )
                sg = sigmoid(summed)
                active = summed * sg
                act_refs[d][lt, pl.ds(r0, BLOCK), :] = active
                if dsil_refs is not None:
                    dsil_refs[d][lt, pl.ds(r0, BLOCK), :] = sg + active * (1.0 - sg)

    over_rows(total, conv_rows)
    out = []
    for d in range(2):
        high, low = split(wide(act_refs[d]))
        sel = pack_ref[0:LANES, :]
        out.append(mm_nt(high, sel) + mm_nt(low, sel))
    return out


def own_front_kernel(dims, pack_ref, sigs_ref, pos_ref, rem_ref, act0_ref, act1_ref, dsil0_ref, dsil1_ref, part_ref,
                     ext_ref):
    parts = conv_silu(dims, 0, sigs_ref, pack_ref, pos_ref, rem_ref, (act0_ref, act1_ref), (dsil0_ref, dsil1_ref),
                      ext_ref)
    for d in range(2):
        part_ref[d] = parts[d]


def front_kernel(dims, *refs):
    n_ch, n_tok, rows, width, chans, inner, rank, states, taps = dims
    total = rows * n_ch
    nt = chans // LANES
    xd = rank + 2 * states
    packs = refs[:n_ch - 1]
    (sigs_ref, pos_ref, rem_ref, part_ref, stepw_hbm, sbias_hbm, picked_ref, stp0_ref, stp1_ref, sgm0_ref, sgm1_ref,
     ext_ref, stepw_pad_ref, pre_ref, act0_ref, act1_ref, stepw_ref, sbias_ref, sems) = refs[n_ch - 1:]
    stp_refs, sgm_refs = (stp0_ref, stp1_ref), (sgm0_ref, sgm1_ref)
    fetches = fetch_all((stepw_hbm, sbias_hbm), (stepw_ref, sbias_ref), sems)
    picked_ref[...] = part_ref[...]
    for k in range(1, n_ch):
        parts = conv_silu(dims, k, sigs_ref, packs[k - 1], pos_ref, rem_ref, (act0_ref, act1_ref), None, ext_ref)
        for d in range(2):
            picked_ref[d] += parts[d]
    for fetch in fetches:
        fetch.wait()
    stepw_pad_ref[...] = jnp.zeros_like(stepw_pad_ref)
    for d in range(2):
        base = d * xd
        stepw_pad_ref[d, base:base + rank, :] = stepw_ref[d]
        pre_ref[...] = mm3(mm, picked_ref[d], stepw_pad_ref[d]) + sbias_ref[d:d + 1, :]

        def step_rows(r0):
            for lt in range(nt):
                x = pre_ref[pl.ds(r0, BLOCK), tile(lt)]
                tail = jnp.exp(-jnp.abs(x))
                whole = 1.0 + tail
                inv = pltpu.reciprocal(whole, approx=True)
                inv = inv * (2.0 - whole * inv)
                small = tail * (1.0 - tail * (0.5 - tail * (1.0 / 3.0)))
                stp_refs[d][lt, pl.ds(r0, BLOCK), :] = jnp.maximum(x, 0.0) + jnp.where(
                    tail < 1e-3, small, jnp.log(whole)
                )
                sgm_refs[d][lt, pl.ds(r0, BLOCK), :] = jnp.where(x >= 0.0, inv, tail * inv)

        over_rows(total, step_rows)


def conv_rows_of(pack_ref, taps):
    return pack_ref[LANES:LANES + 16, :].astype(F32) + pack_ref[LANES + 16:LANES + 32, :].astype(F32)


def selectors(states):
    lanes = np.arange(states * LANES) >> 7
    column = np.arange(LANES)
    spread = ((column[:, None] % states) == lanes[None, :]) & (column[:, None] < 2 * states)
    gather = lanes[:, None] == column[None, :]
    return jnp.asarray(spread, LOW), jnp.asarray(gather, LOW)


def spread_maps(first, states, picked, lanes_ref, e_ref, dest):
    moved = pltpu.roll(picked, LANES - first, 1)
    high = moved.astype(LOW).astype(F32)
    low = pltpu.roll(moved - high, states, 1)
    spot = lax.broadcasted_iota(jnp.int32, moved.shape, 1)
    lanes_ref[...] = jnp.where(spot < states, high, jnp.where(spot < 2 * states, low, 0.0)).astype(LOW)

    dest[...] = mm(lanes_ref[...], e_ref[...])


def fill_rates(rate, nt, states, r2_ref):
    for lt in range(nt):
        for n in range(states):
            r2_ref[lt, n] = jnp.broadcast_to(rate[n:n + 1, tile(lt)] * LOG2E, (8, LANES))


def gate_kernel(dims, *refs):
    n_ch, n_tok, rows, width, chans, inner, rank, states, taps = dims
    total = rows * n_ch
    cots = refs[:n_ch]
    wout_ref, gate_ref, _, cotp_ref, gg_ref, gy_ref = refs[n_ch:]
    me = lax.axis_index("ch")
    for r0 in range(0, total, 256):
        cotp = 0.0
        for k in range(n_ch):
            moved = order_matrix(r0, 256, lax.rem(me + k, n_ch) * rows, rows, total)
            cotp = cotp + mm(moved, cots[k][...])
        cotp_ref[r0:r0 + 256, :] = cotp.astype(LOW)
    gg_ref[...] = mm_nt(cotp_ref[...], wout_ref[...]).astype(LOW)

    def gate_rows(r0):
        rr = pl.ds(r0, BLOCK)
        for lt in range(chans // LANES):
            gate = gate_ref[rr, tile(lt)].astype(F32)
            gy_ref[lt, rr, :] = gg_ref[rr, tile(lt)].astype(F32) * (gate * sigmoid(gate)) * 0.5

    over_rows(total, gate_rows)


def forward_kernel(dims, d, gy_ref, act_ref, stp_ref, picked_ref, dlog_ref, place_ref, e_ref, er_ref, *refs):
    n_ch, n_tok, rows, width, chans, inner, rank, states, taps = dims
    total = rows * n_ch
    length = total // 8
    nt = chans // LANES
    xd = rank + 2 * states
    first = d * xd + rank
    (y_ref, gains_ref, bb_ref, cb_ref, a_ref, h_ref, gmap_ref,
     r2_ref, lanes_ref, p_ref) = refs
    zero = jnp.zeros((8, LANES), F32)
    fill_rates(-jnp.exp(dlog_ref[d]), nt, states, r2_ref)
    spread_maps(first, states, picked_ref[d], lanes_ref, e_ref, bb_ref)
    spread_maps(first + states, states, picked_ref[d], lanes_ref, e_ref, cb_ref)
    p_ref[...] = jnp.zeros_like(p_ref)

    def along(j):
        return pl.multiple_of((length - 1 - j if d else j) * 8, 8)

    def scan_tile(lt, carry):
        def ends(j2, state):
            state, step_sum = list(state[:-1]), state[-1]
            at = [along(2 * j2 + jj) for jj in range(2)]
            sk, u = [], []
            for r0 in at:
                step = stp_ref[lt, pl.ds(r0, 8), :]
                sk.append(jnp.where(place_ref[pl.ds(r0, 8), :] == 0, HUGE_STEP, step))
                u.append(step * act_ref[lt, pl.ds(r0, 8), :])
            for n in range(states):
                for jj, r0 in enumerate(at):
                    a = jnp.exp2(sk[jj] * r2_ref[lt, n])
                    a_ref[lt, pl.ds(r0, 8), lane(n)] = a
                    state[n] = a * state[n] + u[jj] * bb_ref[pl.ds(r0, 8), lane(n)]
            return tuple(state) + (step_sum + (sk[0] + sk[1]),)

        out = over_pairs(length, ends, (zero,) * (states + 1))
        begin = []
        for n in range(states):
            whole_gain = jnp.exp2(out[-1] * r2_ref[lt, n])
            gains_ref[lt, n] = whole_gain
            begin.append(link_blocks(whole_gain, out[n], d == 0))

        def forward(j2, state):
            state = list(state)
            at = [along(2 * j2 + jj) for jj in range(2)]
            r16 = pl.multiple_of((length - 2 - 2 * j2 if d else 2 * j2) * 8, 16)
            u = [stp_ref[lt, pl.ds(r0, 8), :] * act_ref[lt, pl.ds(r0, 8), :] for r0 in at]
            gy = [gy_ref[lt, pl.ds(r0, 8), :] for r0 in at]
            sums = [[None, None], [None, None]]
            for n in range(states):
                prods = []
                for jj, r0 in enumerate(at):
                    h_ref[lt, pl.ds(r0, 8), lane(n)] = state[n]
                    state[n] = a_ref[lt, pl.ds(r0, 8), lane(n)] * state[n] + u[jj] * bb_ref[pl.ds(r0, 8), lane(n)]
                    term = state[n] * cb_ref[pl.ds(r0, 8), lane(n)]
                    sums[jj][n % 2] = term if sums[jj][n % 2] is None else sums[jj][n % 2] + term
                    prods.append(state[n] * gy[jj])
                p_ref[pl.ds(r16, 16), lane(n)] += jnp.concatenate(prods[::-1] if d else prods, axis=0).astype(LOW)
            for jj, r0 in enumerate(at):
                y_ref[lt, pl.ds(r0, 8), :] = sums[jj][0] + sums[jj][1]
            return tuple(state)

        over_pairs(length, forward, tuple(begin))
        return carry

    lax.fori_loop(0, nt, scan_tile, 0)
    gmap_ref[...] = pltpu.roll(mm(p_ref[...], er_ref[...]), first + states, 1)


def out_kernel(dims, y0_ref, y1_ref, act0_ref, act1_ref, skip_ref, gate_ref, gg_ref, normed_ref, cotp_ref, *refs):
    n_ch, n_tok, rows, width, chans, inner, rank, states, taps = dims
    total = rows * n_ch
    gated_ref, ggate_ref, own_ref, send_ref = refs

    def gate_back(r0):
        rr = pl.ds(r0, BLOCK)
        for lt in range(chans // LANES):
            sl = tile(lt)
            out = (
                y0_ref[lt, rr, :] + y1_ref[lt, rr, :]
                + skip_ref[0:1, sl] * act0_ref[lt, rr, :] + skip_ref[1:2, sl] * act1_ref[lt, rr, :]
            ) * 0.5
            gate = gate_ref[rr, sl].astype(F32)
            sg = sigmoid(gate)
            silu = gate * sg
            gated_ref[rr, sl] = (out * silu).astype(LOW)
            ggate_ref[rr, sl] = (gg_ref[rr, sl].astype(F32) * out * (sg + silu * (1.0 - sg))).astype(LOW)

    over_rows(total, gate_back)
    gated = gated_ref[...]
    gout = mm_tn(gated, cotp_ref[...])
    gin = mm_tn(normed_ref[...], ggate_ref[...])
    folded = [gout[:, i * chans:(i + 1) * chans] for i in range(width // chans)]
    pack(own_ref, send_ref, [folded, [gin]])


def block_kernel(dims, gated_ref, wout_ref, _, own_ref, *refs):
    n_ch, rows = dims[0], dims[2]
    part = mm(gated_ref[...], wout_ref[...])
    token_rows(lax.axis_index("ch"), part, n_ch, rows, rows * n_ch, own_ref, refs)


def token_rows(me, part, n_ch, rows, total, own_ref, other_refs):
    high, low = split(part)
    mine = take_tokens(me * rows, rows, total)
    own_ref[...] = mm(mine, high) + mm(mine, low)
    for k in range(1, n_ch):
        theirs = take_tokens(lax.rem(me + k, n_ch) * rows, rows, total)
        other_refs[k - 1][...] = mm(theirs, high).astype(LOW)


def my_place():
    tok = lax.axis_index("tok")
    return tok & 1, (tok >> 1) & 1


def pack(own_ref, send_ref, groups):
    core, near = my_place()
    runs = []
    at = 0
    for group in groups:
        total = sum(piece.shape[0] for piece in group)
        size = chunk_rows(PIECES, total)
        place = 0
        for piece in group:
            for i in range(0, piece.shape[0], 8):
                runs.append(divmod(place + i, size) + (at, piece[i:i + 8, :]))
            place += piece.shape[0]
        for i in range(place, size * PIECES, 8):
            runs.append(divmod(i, size) + (at, jnp.zeros((8, own_ref.shape[2]), F32)))
        at += size
    for side in range(2):
        @pl.when(core == side)
        def _():
            for p, r, base, rows in runs:
                slot = (p & 1) ^ near
                if p >> 1 == side:
                    own_ref[slot, base + r:base + r + 8, :] = rows
                else:
                    send_ref[slot, base + r:base + r + 8, :] = rows.astype(LOW)


def backward_kernel(dims, d, lt, n_wait, *refs):
    n_ch, n_tok, rows, width, chans, inner, rank, states, taps = dims
    total = rows * n_ch
    length = total // 8
    xd = rank + 2 * states
    base = d * xd
    first = base + rank
    sl = tile(lt)
    last_tile = lt == chans // LANES - 1
    refs = list(refs)

    def take(n):
        out = refs[:n]
        del refs[:n]
        return out

    (gy_ref, act_ref, stp_ref, sgm_ref, picked_ref, gains_ref, bb_ref, cb_ref, a_ref, h_ref, dlog_ref, skip_ref,
     stepw_ref, er_ref) = take(14)
    before = take(2)
    take(n_wait)
    gpick_ref, = take(1)
    if last_tile:
        low_ref, = take(1)
    else:
        q_ref, = take(1)
    gact_ref, gstepw_ref, gdlog_ref, misc_ref = take(4)
    if last_tile:
        q_ref, = take(1)
    r2_ref, gu_ref, gs_ref, gpre_ref, stepw_pad_ref = refs

    rate = -jnp.exp(dlog_ref[d, :, sl])
    for n in range(states):
        r2_ref[n] = jnp.broadcast_to(rate[n:n + 1] * LOG2E, (8, LANES))
    zero = jnp.zeros((8, LANES), F32)

    def against(j):
        return pl.multiple_of((j if d else length - 1 - j) * 8, 8)

    def ends_back(j2, state):
        state = list(state)
        at = [against(2 * j2 + jj) for jj in range(2)]
        gy = [gy_ref[lt, pl.ds(r0, 8), :] for r0 in at]
        for n in range(states):
            for jj, r0 in enumerate(at):
                state[n] = a_ref[lt, pl.ds(r0, 8), lane(n)] * (cb_ref[pl.ds(r0, 8), lane(n)] * gy[jj] + state[n])
        return tuple(state)

    back = over_pairs(length, ends_back, (zero,) * states)
    begin = [link_blocks(gains_ref[lt, n], back[n], d == 1) for n in range(states)]

    def backward(j2, state):
        grad, rate_sum = list(state[:states]), list(state[states:])
        at = [against(2 * j2 + jj) for jj in range(2)]
        r16 = pl.multiple_of((2 * j2 if d else length - 2 - 2 * j2) * 8, 16)
        gy = [gy_ref[lt, pl.ds(r0, 8), :] for r0 in at]
        step = [stp_ref[lt, pl.ds(r0, 8), :] for r0 in at]
        u = [step[jj] * act_ref[lt, pl.ds(r0, 8), :] for jj, r0 in enumerate(at)]
        gu = [[None, None], [None, None]]
        gs = [[None, None], [None, None]]
        for n in range(states):
            prods = []
            for jj, r0 in enumerate(at):
                g = cb_ref[pl.ds(r0, 8), lane(n)] * gy[jj] + grad[n]
                prods.append(g * u[jj])
                term = g * bb_ref[pl.ds(r0, 8), lane(n)]
                gu[jj][n % 2] = term if gu[jj][n % 2] is None else gu[jj][n % 2] + term
                grad[n] = a_ref[lt, pl.ds(r0, 8), lane(n)] * g
                q = grad[n] * h_ref[lt, pl.ds(r0, 8), lane(n)]
                rate_sum[n] = rate_sum[n] + q * step[jj]
                term = q * r2_ref[n]
                gs[jj][n % 2] = term if gs[jj][n % 2] is None else gs[jj][n % 2] + term
            value = jnp.concatenate(prods if d else prods[::-1], axis=0).astype(LOW)
            if lt:
                value = value + before[1][pl.ds(r16, 16), lane(n)]
            q_ref[pl.ds(r16, 16), lane(n)] = value
        for jj, r0 in enumerate(at):
            gu_ref[pl.ds(r0, 8), :] = gu[jj][0] + gu[jj][1]
            gs_ref[pl.ds(r0, 8), :] = gs[jj][0] + gs[jj][1]
        return tuple(grad) + tuple(rate_sum)

    last = over_pairs(length, backward, tuple(begin) + (zero,) * states)
    for n in range(states):
        gdlog_ref[n:n + 1, :] = jnp.sum(last[states + n], axis=0, keepdims=True) * rate[n:n + 1]
    misc_ref[...] = jnp.zeros_like(misc_ref)

    def post_rows(r0):
        rr = pl.ds(r0, BLOCK)
        active = act_ref[lt, rr, :]
        gu = gu_ref[rr, :]
        gy = gy_ref[lt, rr, :]
        gpre = (gs_ref[rr, :] * LN2 + gu * active) * sgm_ref[lt, rr, :]
        gpre_ref[rr, :] = gpre
        gact_ref[rr, :] = gu * stp_ref[lt, rr, :] + skip_ref[d:d + 1, sl] * gy
        misc_ref[0:1, :] += jnp.sum(gpre, axis=0, keepdims=True)
        misc_ref[1:2, :] += jnp.sum(gy * active, axis=0, keepdims=True)

    over_rows(total, post_rows)
    stepw_pad_ref[...] = jnp.zeros_like(stepw_pad_ref)
    stepw_pad_ref[base:base + rank, :] = stepw_ref[d, :, sl]
    gpre = gpre_ref[...]
    gpick = mm3(mm_nt, gpre, stepw_pad_ref[...]) + before[0][...]
    if last_tile:
        gpick = gpick + pltpu.roll(mm(q_ref[...], er_ref[...]), first, 1)
        low_ref[...] = gpick.astype(LOW)
    gpick_ref[...] = gpick
    gstepw_ref[...] = mm3(mm_tn, picked_ref[d], gpre)[base:base + rank, :]


def conv_back(dims, d, pos_ref, rem_ref, gpick_refs, gact_refs, act_ref, dsil_ref, sigs_ref, pack_ref, gsig_ref,
              gsel_ref, gconv_ref, gcp_ref, ext_ref, gcs_ref):
    n_ch, n_tok, rows, width, chans, inner, rank, states, taps = dims
    total = rows * n_ch
    nt = chans // LANES
    halo = 8 * (taps - 1)
    xd = rank + 2 * states
    gpick = gpick_refs[0][...]
    for k in range(1, n_ch):
        gpick = gpick + gpick_refs[k][...].astype(F32)
    spot = lax.broadcasted_iota(jnp.int32, (total, LANES), 1)
    gpick = jnp.where((spot >= d * xd) & (spot < (d + 1) * xd), gpick, 0.0)
    high, low = split(gpick)
    sel = pack_ref[0:LANES, :]
    gcp_ref[pl.ds(halo, total), :] = mm(high, sel) + mm(low, sel)
    gsel_ref[...] = mm3(mm_tn, gpick, wide(act_ref))[d * xd:(d + 1) * xd, :]
    ext_ref[pl.ds(halo, total), :] = sigs_ref[0].astype(F32)
    halo_fill(ext_ref, total, halo, slice(None))
    gcs_ref[...] = jnp.zeros_like(gcs_ref)
    conv = conv_rows_of(pack_ref, taps)

    def fold8(x):
        out = x[0:8]
        for i in range(8, BLOCK, 8):
            out = out + x[i:i + 8]
        return out

    def conv_rows(r0):
        rr = pl.ds(r0, BLOCK)
        inside = rem_ref[rr, :] if d else pos_ref[rr, :]
        for lt in range(nt):
            sl = tile(lt)
            gc = (gcp_ref[pl.ds(r0 + halo, BLOCK), sl] + gact_refs[lt][rr, :]) * dsil_ref[lt, rr, :]
            gcp_ref[pl.ds(r0 + halo, BLOCK), sl] = gc
            gcs_ref[taps, :, sl] += fold8(gc)
            gcs_ref[taps - 1, :, sl] += fold8(gc * ext_ref[pl.ds(r0 + halo, BLOCK), sl])
            for lag in range(1, taps):
                far = ext_ref[pl.ds(r0 + (halo + 8 * lag if d else halo - 8 * lag), BLOCK), sl]
                gcs_ref[taps - 1 - lag, :, sl] += fold8(jnp.where(inside >= lag, gc * far, 0.0))

    over_rows(total, conv_rows)
    halo_fill(gcp_ref, total, halo, slice(None))

    def signal_rows(r0):
        rr = pl.ds(r0, BLOCK)
        inside = pos_ref[rr, :] if d else rem_ref[rr, :]
        for lt in range(nt):
            sl = tile(lt)
            at = d * (taps + 1)
            summed = conv[at + taps - 1:at + taps, sl] * gcp_ref[pl.ds(r0 + halo, BLOCK), sl]
            for lag in range(1, taps):
                far = gcp_ref[pl.ds(r0 + (halo - 8 * lag if d else halo + 8 * lag), BLOCK), sl]
                summed = summed + conv[at + taps - 1 - lag:at + taps - lag, sl] * jnp.where(inside >= lag, far, 0.0)
            gsig_ref[rr, sl] = summed

    over_rows(total, signal_rows)
    gconv_ref[...] = jnp.zeros_like(gconv_ref)
    for k in range(taps + 1):
        gconv_ref[k:k + 1, :] = jnp.sum(gcs_ref[k], axis=0, keepdims=True)


def first_conv_kernel(dims, n_wait, pos_ref, rem_ref, *refs):
    n_ch, nt = dims[0], dims[4] // LANES
    gpicks, gacts, refs = refs[:n_ch], refs[n_ch:n_ch + nt], refs[n_ch + nt:]
    conv_back(dims, 0, pos_ref, rem_ref, gpicks, gacts, *refs[:4], *refs[4 + n_wait:])


def second_conv_kernel(dims, pos_ref, rem_ref, *refs):
    n_ch, n_tok, rows, width, chans, inner, rank, states, taps = dims
    nt = chans // LANES
    refs = list(refs)

    def take(n):
        out = refs[:n]
        del refs[:n]
        return out

    gpicks, gacts, rest, _ = take(n_ch), take(nt), take(4), take(2)
    gsig0_ref, gsel0_ref, gconv0_ref, normed_ref, ggate_ref, xp_ref, win_ref = take(7)
    tiles = [[take(3) for _ in range(nt)] for _ in range(2)]
    (gsig_ref, own_ref, send_ref, gcp_ref, ext_ref, gcs_ref, gsum_ref, gsel_ref, gconv_ref, small_ref, gain_ref) = refs
    conv_back(dims, 1, pos_ref, rem_ref, gpicks, gacts, *rest, gsum_ref, gsel_ref, gconv_ref, gcp_ref, ext_ref,
              gcs_ref)
    me = lax.axis_index("ch")
    gsig = (gsum_ref[...] + gsig0_ref[...]).astype(LOW)
    gsig_ref[...] = gsig
    gn = grad_normed(dims, me, gsig, ggate_ref, win_ref)
    xp = xp_ref[...].astype(F32)
    scale = lax.rsqrt(jnp.mean(xp * xp, axis=1, keepdims=True) + norm_eps)
    ggain = jnp.sum(gn * xp * scale, axis=0, keepdims=True)
    gin = mm_tn(normed_ref[...], gsig)
    places = small_places(dims)
    small_ref[...] = jnp.zeros_like(small_ref)
    xd = rank + 2 * states
    for d in range(2):
        at = places["select"] + d * xd
        small_ref[at:at + xd, :] = (gsel0_ref, gsel_ref)[d][...]
        conv_ref = (gconv0_ref, gconv_ref)[d]
        at = places["taps"] + d * taps
        small_ref[at:at + taps, :] = conv_ref[0:taps, :]
        small_ref[places["bias"] + d:places["bias"] + d + 1, :] = conv_ref[taps:taps + 1, :]
        for lt in range(nt):
            gstepw_ref, gdlog_ref, misc_ref = tiles[d][lt]
            sl = tile(lt)
            at = places["step"] + d * rank
            small_ref[at:at + rank, sl] = gstepw_ref[...]
            at = places["decay"] + d * states
            small_ref[at:at + states, sl] = gdlog_ref[...]
            small_ref[places["sbias"] + d:places["sbias"] + d + 1, sl] = misc_ref[0:1, :]
            small_ref[places["skip"] + d:places["skip"] + d + 1, sl] = misc_ref[1:2, :]
    gain_ref[...] = jnp.zeros_like(gain_ref)
    for i in range(width // chans):
        gain_ref[i:i + 1, :] = ggain[:, i * chans:(i + 1) * chans]
    pack(own_ref, send_ref, [[gin], [gain_ref[...]], [small_ref[...]]])


def grad_normed(dims, me, gsig, ggate_ref, win_ref):
    n_ch, n_tok, rows, width, chans, inner, rank, states, taps = dims
    return mm_nt(gsig, win_ref[:, pl.ds(pl.multiple_of(me * chans, LANES), chans)]) + mm_nt(
        ggate_ref[...], win_ref[:, inner:inner + chans]
    )


def normed_kernel(dims, gsig_ref, ggate_ref, win_ref, *refs):
    n_ch, n_tok, rows, width, chans, inner, rank, states, taps = dims
    blk_refs, gn_own_ref, part_refs = refs[:n_ch - 1], refs[n_ch - 1], refs[n_ch:]
    me = lax.axis_index("ch")
    gn = grad_normed(dims, me, gsig_ref[...], ggate_ref, win_ref)
    token_rows(me, gn, n_ch, rows, rows * n_ch, gn_own_ref, [ref.at[rows:2 * rows] for ref in part_refs])
    for blk_ref, part_ref in zip(blk_refs, part_refs):
        part_ref[0:rows, :] = blk_ref[...]


def small_places(dims):
    n_ch, n_tok, rows, width, chans, inner, rank, states, taps = dims
    places, at = {}, 0
    for name, size in (
        ("select", 2 * (rank + 2 * states)), ("step", 2 * rank), ("decay", 2 * states), ("taps", 2 * taps),
        ("bias", 2), ("sbias", 2), ("skip", 2),
    ):
        places[name] = at
        at += size
    places["end"] = round_up(at, 8)
    return places


def token_kernel(n_ch, at, tok_ref, cot_ref, gain_ref, blk_ref, gn_ref, *refs):
    parts = refs[:n_ch - 1]
    out_ref, gtok_ref, mark_ref = refs[n_ch - 1:]
    mark_ref[...] = jnp.zeros_like(mark_ref)
    tokens = tok_ref[...].astype(F32)
    out = tokens + blk_ref[...]
    gn = gn_ref[...]
    rows = tok_ref.shape[0]
    for part in parts:
        out = out + part[at:at + rows, :].astype(F32)
        gn = gn + part[at + rows:at + 2 * rows, :].astype(F32)
    out_ref[...] = out.astype(LOW)
    scale = lax.rsqrt(jnp.mean(tokens * tokens, axis=1, keepdims=True) + norm_eps)
    unit = tokens * scale
    scaled = gn * gain_ref[...][None, :]
    gtok_ref[...] = cot_ref[...].astype(F32) + scale * (
        scaled - unit * jnp.mean(scaled * unit, axis=1, keepdims=True)
    )


def join_kernel(n_ch, rb, base_ref, *refs):
    others, out_ref = refs[:n_ch - 1], refs[-1]
    out_ref[0:rb, :] = base_ref[0:rb, :]
    mixed = base_ref[rb:rb + 16, :].astype(F32)
    gain = mixed[0:8]
    for c, other in enumerate(others):
        out_ref[(c + 1) * rb:(c + 2) * rb, :] = other[0:rb, :]
        gain = gain + other[rb:rb + 16, :].astype(F32)[0:8]
    at = n_ch * rb
    out_ref[at:at + 16, :] = jnp.concatenate([gain, mixed[8:16]], axis=0).astype(LOW)
    out_ref[at + 16:, :] = base_ref[rb + 16:, :]


def my_pieces():
    core, near = my_place()
    return [(core ^ (k >> 1)) * 2 + (near ^ (k & 1)) for k in range(PIECES)]


def place_columns(dims, every, at, block_ref, gin_hbm, first, sems):
    n_ch, n_tok, rows, width, chans, inner, rank, states, taps = dims
    rb = chunk_rows(PIECES, width)
    me = lax.axis_index("ch")
    copies = []
    for k, piece in enumerate(my_pieces()):
        rr = pl.ds(pl.multiple_of(piece * rb, 8), rb)
        for c in range(n_ch):
            j = lax.rem(me + c, n_ch) * chans
            block_ref[k, :, pl.ds(pl.multiple_of(j, LANES), chans)] = every[k][
                at + c * rb:at + (c + 1) * rb, :
            ].astype(F32)
        copies.append(pltpu.make_async_copy(block_ref.at[k], gin_hbm.at[rr, first:first + inner], sems.at[k]))
        copies[-1].start()
    return copies


def early_result_kernel(dims, every_ref, gin_hbm, gout_hbm, mark_ref, block_ref, gout_ref, sems):
    n_ch, n_tok, rows, width, chans, inner, rank, states, taps = dims
    ra = chunk_rows(PIECES, chans)
    copies = place_columns(dims, [every_ref.at[k] for k in range(PIECES)], ra, block_ref, gin_hbm, inner, sems)
    for k, piece in enumerate(my_pieces()):
        gout_ref[pl.ds(pl.multiple_of(piece * ra, 8), ra), :] = every_ref[k, 0:ra, :].astype(F32)
    mark_ref[...] = jnp.zeros_like(mark_ref)
    copies.append(pltpu.make_async_copy(gout_ref, gout_hbm, sems.at[PIECES]))
    copies[-1].start()
    for copy in copies:
        copy.wait()


def late_result_kernel(dims, *refs):
    every, gin_hbm, refs = refs[:PIECES], refs[PIECES + 1], refs[PIECES + 2:]
    n_ch, n_tok, rows, width, chans, inner, rank, states, taps = dims
    outs, stages, (small_ref, block_ref, sems) = refs[:8], refs[8:16], refs[16:]
    ggain_ref, gtaps_ref, gbias_ref, gsel_ref, gstep_ref, gsbias_ref, gdecay_ref, gskip_ref = stages
    places = small_places(dims)
    rb, rs = chunk_rows(PIECES, width), chunk_rows(PIECES, places["end"])
    at = n_ch * rb
    gain = 0.0
    for k, piece in enumerate(my_pieces()):
        mixed = every[k][at:at + 8 + rs, :].astype(F32)
        small_ref[pl.ds(pl.multiple_of(piece * rs, 8), rs), :] = mixed[8:]
        gain = gain + mixed[0:8]
    ggain_ref[...] = gain[0]
    xd = rank + 2 * states
    for d in range(2):
        for ref, name, size in ((gsel_ref, "select", xd), (gstep_ref, "step", rank), (gdecay_ref, "decay", states),
                                (gtaps_ref, "taps", taps)):
            first = places[name] + d * size
            ref[d] = small_ref[first:first + size, :]
    for ref, name in ((gbias_ref, "bias"), (gsbias_ref, "sbias"), (gskip_ref, "skip")):
        ref[...] = small_ref[places[name]:places[name] + 2, :]
    copies = [pltpu.make_async_copy(a, b, sems.at[PIECES + i]) for i, (a, b) in enumerate(zip(stages, outs))]
    for copy in copies:
        copy.start()
    copies += place_columns(dims, every, 0, block_ref, gin_hbm, 0, sems)
    for copy in copies:
        copy.wait()


def chunk_rows(n_tok, total):
    return round_up(-(-total // n_tok), 8)


def vmem_specs(n):
    return [pl.BlockSpec(memory_space=pltpu.VMEM)] * n


def kernel_call(kernel, name, operands, outs, scratch, limit, us, places=(), hbm_outs=(), aliases=()):
    specs = vmem_specs(len(operands))
    for i, space in places:
        specs[i] = pl.BlockSpec(memory_space=space)
    return pl.pallas_call(
        kernel,
        name=name,
        out_shape=outs,
        in_specs=specs,
        out_specs=[pl.BlockSpec(memory_space=pl.ANY if i in hbm_outs else pltpu.VMEM) for i in range(len(outs))],
        scratch_shapes=scratch,
        input_output_aliases=dict(aliases),
        compiler_params=pltpu.CompilerParams(vmem_limit_bytes=limit * 1024 * 1024),
        cost_estimate=pl.CostEstimate(flops=int(us * 1e7), bytes_accessed=int(us * 3e4), transcendentals=0),
    )(*operands)


def rotated(x, n_ch):
    return [x] + [
        lax.ppermute(x, "ch", [((i + k) % n_ch, i) for i in range(n_ch)]) for k in range(1, n_ch)
    ]


def sent(parts, n_ch):
    return [
        lax.ppermute(parts[k - 1], "ch", [(i, (i + k) % n_ch) for i in range(n_ch)]) for k in range(1, n_ch)
    ]


def partner_pairs(n_tok, stride):
    return [(i, i ^ stride) for i in range(n_tok)]


def swap(x, n_tok, stride):
    return lax.ppermute(x, "tok", partner_pairs(n_tok, stride))


def near_strides():
    return [1, 2]


def far_strides(n_tok):
    strides, s = [], 4
    while s < n_tok:
        strides.append(s)
        s *= 2
    return strides


def add_kernel(halving, last, own_ref, got_ref, *refs):
    send_ref = refs[-1]
    if halving:
        refs[-2][...] = own_ref[0] + got_ref[0].astype(F32)
        send_ref[...] = (own_ref[1] + got_ref[1].astype(F32)).astype(LOW)
    else:
        both = own_ref[...] + got_ref[...].astype(F32)
        send_ref[...] = both.astype(LOW)
        if not last:
            refs[-2][...] = both


class Reduction:
    def __init__(self, own, send, n_tok, limit):
        self.own, self.n_tok, self.limit = own, n_tok, limit
        self.strides = [2] + far_strides(n_tok)
        self.got = swap(send, n_tok, 1)

    def done(self):
        return self.own.dtype == LOW

    def add(self, *wait):
        halving, last = self.own.ndim == 3, not self.strides
        shape = self.own.shape[-2:]
        outs = kernel_call(
            functools.partial(add_kernel, halving, last), "add_kernel", (self.own, self.got, *wait),
            ([] if last else [jax.ShapeDtypeStruct(shape, F32)]) + [jax.ShapeDtypeStruct(shape, LOW)], [], self.limit,
            0.1, [(i, pl.ANY) for i in range(2, 2 + len(wait))],
        )
        self.own = outs[0]
        if not last:
            self.got = swap(outs[1], self.n_tok, self.strides.pop(0))


def stack_kernel(spans, *refs):
    at = 0
    for (first, rows), ref in zip(spans, refs):
        refs[-1][at:at + rows, :] = ref[first:first + rows, :]
        at += rows


def stack(parts, wait, limit):
    parts = [part if isinstance(part, tuple) else (part, 0, part.shape[0]) for part in parts]
    arrays, spans = [part[0] for part in parts], [part[1:] for part in parts]
    shape = (sum(rows for _, rows in spans), arrays[0].shape[1])
    return kernel_call(
        functools.partial(stack_kernel, spans), "stack_kernel", (*arrays, wait), [jax.ShapeDtypeStruct(shape, LOW)], [],
        limit, 0.1, [(len(parts), pl.ANY)],
    )[0]


def local(
    tokens,
    cotangent,
    norm_gain,
    in_proj,
    conv_weight,
    conv_bias,
    select_proj,
    step_proj,
    step_bias,
    decay_log,
    skip_gain,
    out_proj,
    clip_lengths,
):
    n_ch, n_tok = lax.axis_size("ch"), lax.axis_size("tok")
    rows, width = tokens.shape
    real = conv_bias.shape[1]
    taps, rank, states = conv_weight.shape[1], step_proj.shape[1], decay_log.shape[1]
    chans = round_up(real, LANES)
    extra = chans - real
    xd = rank + 2 * states

    def pad_last(x):
        return jnp.pad(x, [(0, 0)] * (x.ndim - 1) + [(0, extra)]) if extra else x

    if extra:
        in_proj = pad_last(in_proj.reshape(width, 2 * n_ch, real)).reshape(width, 2 * n_ch * chans)
        step_proj, step_bias, decay_log, skip_gain = map(pad_last, (step_proj, step_bias, decay_log, skip_gain))
        out_proj = jnp.pad(out_proj, ((0, extra), (0, 0)))
    inner = n_ch * chans
    total = rows * n_ch
    nt = chans // LANES
    span = states * LANES
    halo = 8 * (taps - 1)
    fold = width // chans
    dims = (n_ch, n_tok, rows, width, chans, inner, rank, states, taps)
    limit = 16 if total <= 256 else 60
    shape = jax.ShapeDtypeStruct
    vm = pltpu.VMEM
    one = (nt, total, LANES)
    dma = pltpu.SemaphoreType.DMA
    spot = shape((total, LANES), jnp.int32)

    def far(*arrays):
        return [pltpu.with_memory_space_constraint(x, pltpu.HBM) for x in arrays]

    tok_parts = rotated(tokens, n_ch)
    (packed,) = kernel_call(
        functools.partial(weight_kernel, dims), "weight_kernel",
        far(select_proj.transpose(0, 2, 1), conv_weight, conv_bias), [shape((LANES + 32, chans), LOW)],
        [vm((2, xd, real), F32), vm((2, taps, real), F32), vm((2, real), F32), dma((3,))], limit, 20,
        [(i, pltpu.HBM) for i in range(3)],
    )
    pack_parts = rotated(packed, n_ch)
    fetched = (in_proj, tokens, norm_gain, cotangent)
    win, own, gain, cot_own = kernel_call(
        functools.partial(fetch_kernel, inner, chans), "fetch_kernel", (*far(*fetched), packed),
        [shape((width, inner + chans), LOW)] + [shape(x.shape, x.dtype) for x in fetched[1:]], [dma((5,))], limit, 20,
        [(i, pltpu.HBM) for i in range(len(fetched))] + [(len(fetched), pl.ANY)],
    )
    normed, xp, sigs, gate, pos, rem = kernel_call(
        functools.partial(norm_kernel, dims), "norm_kernel",
        (*far(clip_lengths), own, gain, win, *tok_parts[1:]),
        [shape((total, width), LOW), shape((total, width), LOW), shape((n_ch, total, chans), LOW),
         shape((total, chans), LOW), spot, spot],
        [pltpu.SMEM(clip_lengths.shape, jnp.int32), dma], limit, 50, [(0, pltpu.HBM)],
    )
    cot_parts = rotated(cot_own, n_ch)
    ext = vm((total + 2 * halo, chans), F32)
    act0, act1, dsil0, dsil1, part = kernel_call(
        functools.partial(own_front_kernel, dims), "own_front_kernel", (packed, sigs, pos, rem),
        [shape(one, F32)] * 4 + [shape((2, total, LANES), F32)], [ext], limit, 1,
    )
    picked, stp0, stp1, sgm0, sgm1 = kernel_call(
        functools.partial(front_kernel, dims), "front_kernel",
        (*pack_parts[1:], sigs, pos, rem, part, *far(step_proj, step_bias)),
        [shape((2, total, LANES), F32)] + [shape(one, F32)] * 4,
        [ext, vm((2, LANES, chans), F32), vm((total, chans), F32), vm(one, F32), vm(one, F32),
         vm((2, rank, chans), F32), vm((2, chans), F32), dma((2,))],
        limit, 1, ((n_ch + 3, pltpu.HBM), (n_ch + 4, pltpu.HBM)),
    )

    ra, rb = chunk_rows(PIECES, chans * fold), chunk_rows(PIECES, width)
    r1 = ra + rb
    cotp, gg, gy = kernel_call(
        functools.partial(gate_kernel, dims), "gate_kernel", (*cot_parts, out_proj, gate, picked),
        [shape((total, width), LOW), shape((total, chans), LOW), shape(one, F32)], [], limit, 1,
        [(n_ch + 2, pl.ANY)],
    )
    spread, gather = selectors(states)
    scans = []
    for d, (act, stp) in enumerate(((act0, stp0), (act1, stp1))):
        scans.append(kernel_call(
            functools.partial(forward_kernel, dims, d), "forward_kernel_%d" % d,
            (gy, act, stp, picked, decay_log, rem if d else pos, spread, gather),
            [shape(one, F32), shape((nt, states, 8, LANES), F32)] + [shape((total, span), F32)] * 2
            + [shape((nt, total, span), F32)] * 2 + [shape((total, LANES), F32)],
            [vm((nt, states, 8, LANES), F32), vm((total, LANES), LOW), vm((total, span), LOW)],
            limit, 1,
        ))
    outs = kernel_call(
        functools.partial(out_kernel, dims), "out_kernel",
        (scans[0][0], scans[1][0], act0, act1, skip_gain, gate, gg, normed, cotp),
        [shape((total, chans), LOW), shape((total, chans), LOW), shape((2, r1, chans), F32),
         shape((2, r1, chans), LOW)],
        [], limit, 1,
    )
    gated, ggate, own1, send1 = outs

    early = Reduction(own1, send1, n_tok, limit)
    gpick_parts, gacts, tile_outs = [], [], [[], []]
    for d, (act, stp, sgm) in enumerate(((act0, stp0, sgm0), (act1, stp1, sgm1))):
        gains, bb, cb, decays, before_states, gmap = scans[d][1:]
        before = (gmap, gmap)
        gacts.append([])
        for lt in range(nt):
            final = lt == nt - 1
            operands = (gy, act, stp, sgm, picked, gains, bb, cb, decays, before_states, decay_log, skip_gain,
                        step_proj, gather, *before)
            wait = [early.own] if (d, lt) in ((1, 0), (1, nt - 1)) else []
            outs = kernel_call(
                functools.partial(backward_kernel, dims, d, lt, len(wait)), "backward_kernel_%d%d" % (d, lt),
                (*operands, *wait),
                [shape((total, LANES), F32)]
                + ([shape((total, LANES), LOW)] if final else [shape((total, span), LOW)])
                + [shape((total, LANES), F32), shape((rank, LANES), F32), shape((states, LANES), F32),
                   shape((8, LANES), F32)],
                ([vm((total, span), LOW)] if final else [])
                + [vm((states, 8, LANES), F32), vm((total, LANES), F32), vm((total, LANES), F32),
                   vm((total, LANES), F32), vm((LANES, LANES), F32)],
                limit, 0.5, [(len(operands) + i, pl.ANY) for i in range(len(wait))],
            )
            before = tuple(outs[:2])
            gacts[d].append(outs[2])
            tile_outs[d].extend(outs[-3:])
            if early.strides and (d, lt) in ((0, 0), (0, nt - 1), (1, nt - 2)):
                early.add(outs[-1])
        gpick_parts.append([outs[0]] + rotated(outs[1], n_ch)[1:])

    wait = [tile_outs[1][-1]]
    conv_scratch = [vm((total + 2 * halo, chans), F32), vm((total + 2 * halo, chans), F32),
                    vm((taps + 1, 8, chans), F32)]
    operands = (pos, rem, *gpick_parts[0], *gacts[0], act0, dsil0, sigs, packed, *wait)
    gsig0, gsel0, gconv0 = kernel_call(
        functools.partial(first_conv_kernel, dims, len(wait)), "first_conv_kernel", operands,
        [shape((total, chans), F32), shape((xd, chans), F32), shape((8, chans), F32)],
        conv_scratch, limit, 0.5, [(i, pl.ANY) for i in range(len(operands) - len(wait), len(operands))],
    )
    outs = kernel_call(
        functools.partial(block_kernel, dims), "block_kernel", (gated, out_proj, gconv0),
        [shape((rows, width), F32)] + [shape((rows, width), LOW)] * (n_ch - 1), [], limit, 0.5, [(2, pl.ANY)],
    )
    blk_own, blk_parts = outs[0], outs[1:]
    places = small_places(dims)
    rs = chunk_rows(PIECES, places["end"])
    r2 = rs + rb + 8
    gsig, own2, send2 = kernel_call(
        functools.partial(second_conv_kernel, dims), "second_conv_kernel",
        (pos, rem, *gpick_parts[1], *gacts[1], act1, dsil1, sigs, packed, blk_own, early.got, gsig0, gsel0, gconv0, normed, ggate, xp,
         win, *tile_outs[0], *tile_outs[1]),
        [shape((total, chans), LOW), shape((2, r2, chans), F32), shape((2, r2, chans), LOW)],
        conv_scratch + [vm((total, chans), F32), vm((xd, chans), F32), vm((8, chans), F32),
                        vm((places["end"], chans), F32), vm((8, chans), F32)],
        limit, 0.5, [(6 + n_ch + nt, pl.ANY), (7 + n_ch + nt, pl.ANY)],
    )
    outs = kernel_call(
        functools.partial(normed_kernel, dims), "normed_kernel", (gsig, ggate, win, *blk_parts),
        [shape((rows, width), F32)] + [shape((2 * rows, width), LOW)] * (n_ch - 1), [], limit, 0.5,
    )
    gn_own, token_parts = outs[0], outs[1:n_ch]

    late = Reduction(own2, send2, n_tok, limit)
    early.add(gn_own)
    while not early.done():
        early.add()
    gate = (early.own, ra, rb)
    if n_ch == 2 and width == chans:
        token_got = gates = sent([stack([gate, token_parts[0]], gn_own, limit)], n_ch)
    else:
        token_got, gates = sent(token_parts, n_ch), rotated(early.own[ra:], n_ch)[1:]
    late.add(gn_own)
    late.add()
    block_out, grad_tokens, mark = kernel_call(
        functools.partial(token_kernel, n_ch, token_got[0].shape[0] - 2 * rows), "token_kernel",
        (own, cot_own, gain, blk_own, gn_own, *token_got),
        [shape((rows, width), LOW), shape((rows, width), F32), shape((8, LANES), F32)], [], limit, 0.5,
    )
    early_piece = stack([early.own, *((got, 0, rb) for got in gates)], mark, limit)
    first_got = swap(early_piece, n_tok, 2)
    late.add(mark)
    while not late.done():
        late.add()
    early_pair = stack([early_piece, first_got], late.own, limit).reshape(2, ra + n_ch * rb, chans)
    every1 = jnp.concatenate([early_pair, swap(early_pair, n_tok, 1)], axis=0)
    assert rb % 16 == 0 and (rs + 8) % 16 == 0
    shared = late.own[:rb + 16]
    sides = [[], []]
    for side in range(2):
        for c in range(n_ch):
            if (side, c) == (0, 0):
                sides[0].append(late.own)
                continue
            pairs = [
                ((i ^ (2 * side)) * n_ch + (j + c) % n_ch, i * n_ch + j) for i in range(n_tok) for j in range(n_ch)
            ]
            sides[side].append(lax.ppermute(shared if c else late.own, ("tok", "ch"), pairs))

    def join(wait):
        mine = [
            kernel_call(
                functools.partial(join_kernel, n_ch, rb), "join_kernel", (*parts, wait),
                [shape((n_ch * rb + 8 + rs, chans), LOW)], [], limit, 0.5, [(n_ch, pl.ANY)],
            )[0] for parts in sides
        ]
        return mine + [swap(piece, n_tok, 1) for piece in mine]

    if not extra and fold == 1 and ra * PIECES == chans and rb * PIECES == width:
        block = vm((PIECES, rb, inner), F32)
        gin, gout, mark = kernel_call(
            functools.partial(early_result_kernel, dims), "early_result_kernel", (every1,),
            [shape((width, 2 * inner), F32), shape((chans, width), F32), shape((8, LANES), F32)],
            [block, vm((chans, width), F32), dma((PIECES + 1,))], limit, 2, hbm_outs=(0, 1),
        )
        every2 = join(mark)
        small_shapes = [(width,), (2, taps, chans), (2, chans), (2, xd, chans), (2, rank, chans), (2, chans),
                        (2, states, chans), (2, chans)]
        gin, ggain, gtaps, gbias, gsel, gstep, gsbias, gdecay, gskip = kernel_call(
            functools.partial(late_result_kernel, dims), "late_result_kernel",
            (*every2, gin),
            [shape((width, 2 * inner), F32)] + [shape(x, F32) for x in small_shapes],
            [vm(x, F32) for x in small_shapes] + [vm((rs * PIECES, chans), F32), block, dma((PIECES + 8,))], limit, 2,
            [(PIECES, pl.ANY)], hbm_outs=range(9), aliases={PIECES: 0},
        )
    else:
        every2 = jnp.stack(join(late.own))
        me, tok = lax.axis_index("ch"), lax.axis_index("tok")
        mine = (tok & 1) * 2 + ((tok >> 1) & 1)
        at = jnp.arange(PIECES) ^ mine
        every1, every2 = every1[at], every2[at]
        turn = (jnp.arange(n_ch) - me) % n_ch
        gate = every1[:, ra:].reshape(PIECES, n_ch, rb, chans)
        signal = every2[:, :n_ch * rb].reshape(PIECES, n_ch, rb, chans)
        gin = jnp.concatenate([signal[:, turn], gate[:, turn]], axis=1).transpose(0, 2, 1, 3)[..., :real]
        gin = gin.reshape(PIECES * rb, 2 * n_ch * real)[:width].astype(F32)
        gout = every1[:, :ra].reshape(PIECES * ra, chans)[:chans * fold]
        gout = jnp.concatenate([gout[i * chans:(i + 1) * chans] for i in range(fold)], axis=1)[:real].astype(F32)
        small = every2[:, n_ch * rb + 8:].reshape(PIECES * rs, chans).astype(F32)
        ggain = jnp.sum(every2[:, n_ch * rb:n_ch * rb + 8].astype(F32), axis=0)[:fold].reshape(width)

        def rows_of(name, size):
            return small[places[name]:places[name] + size]

        gsel, gstep, gdecay, gtaps = (
            rows_of(name, 2 * size).reshape(2, size, chans)[..., :real]
            for name, size in (("select", xd), ("step", rank), ("decay", states), ("taps", taps))
        )
        gbias, gsbias, gskip = (rows_of(name, 2)[:, :real] for name in ("bias", "sbias", "skip"))
    return (
        block_out,
        grad_tokens,
        ggain,
        gin,
        gtaps,
        gbias,
        gsel.transpose(0, 2, 1),
        gstep,
        gsbias,
        gdecay,
        gskip,
        gout,
    )


def solution(mesh):
    return jax.shard_map(
        local,
        mesh=mesh,
        in_specs=(
            P(("tok", "ch"), None),
            P(("tok", "ch"), None),
            P(),
            P(),
            P(None, None, "ch"),
            P(None, "ch"),
            P(None, "ch", None),
            P(None, None, "ch"),
            P(None, "ch"),
            P(None, None, "ch"),
            P(None, "ch"),
            P("ch", None),
            P("tok", None),
        ),
        out_specs=(
            P(("tok", "ch"), None),
            P(("tok", "ch"), None),
            P(),
            P(),
            P(None, None, "ch"),
            P(None, "ch"),
            P(None, "ch", None),
            P(None, None, "ch"),
            P(None, "ch"),
            P(None, None, "ch"),
            P(None, "ch"),
            P("ch", None),
        ),
        check_vma=False,
    )
```

```python
import functools
import math

import jax
import jax.numpy as jnp
import numpy as np
from jax import lax
from jax.experimental import pallas as pl
from jax.experimental.pallas import tpu as pltpu
from jax.sharding import PartitionSpec as P

norm_eps = 1e-05
F32 = jnp.float32
LOW = jnp.bfloat16
LANES = 128
HUGE_STEP = 1e30
LOG2E = math.log2(math.e)
LN2 = math.log(2.0)
BLOCK = 256
PAIRS = 8
PIECES = 4


def mm(a, b):
    return lax.dot_general(a, b, (((1,), (0,)), ((), ())), preferred_element_type=F32)


def mm_nt(a, b):
    return lax.dot_general(a, b, (((1,), (1,)), ((), ())), preferred_element_type=F32)


def mm_tn(a, b):
    return lax.dot_general(a, b, (((0,), (0,)), ((), ())), preferred_element_type=F32)


def split(x):
    high = x.astype(LOW)
    return high, (x - high.astype(F32)).astype(LOW)


def mm3(dot, a, b):
    a_high, a_low = split(a)
    b_high, b_low = split(b)
    return dot(a_high, b_high) + (dot(a_high, b_low) + dot(a_low, b_high))


def round_up(x, m):
    return -(-x // m) * m


def wide(ref, *lead):
    parts = [ref[lead + (i,)] for i in range(ref.shape[len(lead)])]
    return parts[0] if len(parts) == 1 else jnp.concatenate(parts, axis=-1)


def row_time(r, length):
    return (r & 7) * length + (r >> 3)


def clip_places(len_ref, total, shape):
    t = row_time(lax.broadcasted_iota(jnp.int32, shape, 0), total // 8)
    clips = len_ref.shape[1]
    ends = []
    acc = 0
    for c in range(clips):
        acc = acc + len_ref[0, c]
        ends.append(acc)
    start = jnp.zeros(shape, jnp.int32)
    end = jnp.full(shape, total, jnp.int32)
    for c in range(clips - 1):
        start = jnp.where(t >= ends[c], ends[c], start)
    for c in range(clips - 2, -1, -1):
        end = jnp.where(t < ends[c], ends[c], end)
    return t - start, end - 1 - t


def order_matrix(first, rows, first_token, tokens, total):
    r = lax.broadcasted_iota(jnp.int32, (rows, tokens), 0) + first
    t = lax.broadcasted_iota(jnp.int32, (rows, tokens), 1) + first_token
    return jnp.where(row_time(r, total // 8) == t, 1.0, 0.0).astype(LOW)


def take_tokens(first, rows, total):
    t = lax.broadcasted_iota(jnp.int32, (rows, total), 0) + first
    r = lax.broadcasted_iota(jnp.int32, (rows, total), 1)
    return jnp.where(row_time(r, total // 8) == t, 1.0, 0.0).astype(LOW)


def halo_fill(ext_ref, total, halo, sl):
    for q in range(halo // 8):
        tail = ext_ref[pl.ds(total + 8 * q, 8), sl]
        ext_ref[pl.ds(8 * q, 8), sl] = pltpu.roll(tail, 1, 0)
        head = ext_ref[pl.ds(halo + 8 * q, 8), sl]
        ext_ref[pl.ds(halo + total + 8 * q, 8), sl] = pltpu.roll(head, 7, 0)


def link_blocks(gain, added, toward_end):
    row = lax.broadcasted_iota(jnp.int32, gain.shape, 0)
    for k in (1, 2, 4):
        shift = k if toward_end else 8 - k
        inside = (row >= k) if toward_end else (row < 8 - k)
        added_near = jnp.where(inside, pltpu.roll(added, shift, 0), 0.0)
        gain_near = jnp.where(inside, pltpu.roll(gain, shift, 0), 1.0)
        added = added + gain * added_near
        gain = gain * gain_near
    if toward_end:
        return jnp.where(row >= 1, pltpu.roll(added, 1, 0), 0.0)
    return jnp.where(row < 7, pltpu.roll(added, 7, 0), 0.0)


def over_rows(total, body):
    def step(i, carry):
        body(pl.multiple_of(i * BLOCK, BLOCK))
        return carry

    lax.fori_loop(0, total // BLOCK, step, 0)


def over_pairs(length, body, init):
    def trip(i, carry):
        for q in range(PAIRS):
            carry = body(i * PAIRS + q, carry)
        return carry

    return lax.fori_loop(0, length // 2 // PAIRS, trip, init)


def tile(lt):
    return slice(lt * LANES, (lt + 1) * LANES)


def lane(n):
    return slice(n * LANES, (n + 1) * LANES)


def sigmoid(x):
    return 0.5 * jnp.tanh(0.5 * x) + 0.5


def fetch_all(sources, targets, sems):
    copies = [pltpu.make_async_copy(a, b, sems.at[i]) for i, (a, b) in enumerate(zip(sources, targets))]
    for copy in copies:
        copy.start()
    return copies


def weight_kernel(dims, select_hbm, taps_hbm, bias_hbm, packed_ref, select_ref, taps_ref, bias_ref, sems):
    taps, real = taps_ref.shape[1:]
    xd = select_ref.shape[1]
    for copy in fetch_all((select_hbm, taps_hbm, bias_hbm), (select_ref, taps_ref, bias_ref), sems):
        copy.wait()
    parts = [select_ref[0], select_ref[1], jnp.zeros((LANES - 2 * xd, real), F32)]
    packed_ref[0:LANES, 0:real] = jnp.concatenate(parts, axis=0).astype(LOW)
    parts = []
    for d in range(2):
        parts += [taps_ref[d], bias_ref[d:d + 1, :]]
    parts.append(jnp.zeros((16 - 2 * (taps + 1), real), F32))
    high, low = split(jnp.concatenate(parts, axis=0))
    packed_ref[LANES:LANES + 16, 0:real] = high
    packed_ref[LANES + 16:LANES + 32, 0:real] = low
    if real < packed_ref.shape[1]:
        packed_ref[:, real:] = jnp.zeros((LANES + 32, packed_ref.shape[1] - real), LOW)


def fetch_kernel(inner, chans, win_hbm, own_hbm, gain_hbm, cot_hbm, _, win_ref, own_ref, gain_ref, cot_ref, sems):
    first = pl.multiple_of(inner + lax.axis_index("ch") * chans, LANES)
    for copy in fetch_all(
        (win_hbm.at[:, 0:inner], win_hbm.at[:, pl.ds(first, chans)], own_hbm, gain_hbm, cot_hbm),
        (win_ref.at[:, 0:inner], win_ref.at[:, inner:inner + chans], own_ref, gain_ref, cot_ref), sems,
    ):
        copy.wait()


def norm_kernel(dims, len_hbm, own_ref, gain_ref, win_ref, *refs):
    n_ch, n_tok, rows, width, chans, inner, rank, states, taps = dims
    total = rows * n_ch
    toks = [own_ref, *refs[:n_ch - 1]]
    normed_ref, xp_ref, sigs_ref, gate_ref, pos_ref, rem_ref, len_ref, sem = refs[n_ch - 1:]
    me = lax.axis_index("ch")
    fetch = pltpu.make_async_copy(len_hbm, len_ref, sem)
    fetch.start()
    gain = gain_ref[...][None, :]
    for r0 in range(0, total, 256):
        rr = slice(r0, r0 + 256)
        xp = 0.0
        for k in range(n_ch):
            xp = xp + mm(order_matrix(r0, 256, lax.rem(me + k, n_ch) * rows, rows, total), toks[k][...])
        xp_ref[rr, :] = xp.astype(LOW)
        scale = lax.rsqrt(jnp.mean(xp * xp, axis=1, keepdims=True) + norm_eps)
        normed_ref[rr, :] = (xp * scale * gain).astype(LOW)
    normed = normed_ref[...]
    for k in range(n_ch):
        j = lax.rem(me + k, n_ch)
        sigs_ref[k] = mm(normed, win_ref[:, pl.ds(pl.multiple_of(j * chans, LANES), chans)]).astype(LOW)
    gate_ref[...] = mm(
        normed, win_ref[:, inner:inner + chans]
    ).astype(LOW)
    fetch.wait()
    pos, rem = clip_places(len_ref, total, (total, LANES))
    pos_ref[...] = pos
    rem_ref[...] = rem


def conv_silu(dims, k, sigs_ref, pack_ref, pos_ref, rem_ref, act_refs, dsil_refs, ext_ref):
    n_ch, n_tok, rows, width, chans, inner, rank, states, taps = dims
    total = rows * n_ch
    halo = 8 * (taps - 1)
    ext_ref[pl.ds(halo, total), :] = sigs_ref[k].astype(F32)
    halo_fill(ext_ref, total, halo, slice(None))
    conv = conv_rows_of(pack_ref, taps)

    def conv_rows(r0):
        pos_b = pos_ref[pl.ds(r0, BLOCK), :]
        rem_b = rem_ref[pl.ds(r0, BLOCK), :]
        for lt in range(chans // LANES):
            sl = tile(lt)
            for d in range(2):
                inside = rem_b if d else pos_b
                at = d * (taps + 1)
                summed = conv[at + taps:at + taps + 1, sl] + conv[at + taps - 1:at + taps, sl] * ext_ref[
                    pl.ds(r0 + halo, BLOCK), sl
                ]
                for lag in range(1, taps):
                    far = ext_ref[pl.ds(r0 + (halo + 8 * lag if d else halo - 8 * lag), BLOCK), sl]
                    summed = summed + conv[at + taps - 1 - lag:at + taps - lag, sl] * jnp.where(
                        inside >= lag, far, 0.0
                    )
                sg = sigmoid(summed)
                active = summed * sg
                act_refs[d][lt, pl.ds(r0, BLOCK), :] = active
                if dsil_refs is not None:
                    dsil_refs[d][lt, pl.ds(r0, BLOCK), :] = sg + active * (1.0 - sg)

    over_rows(total, conv_rows)
    out = []
    for d in range(2):
        high, low = split(wide(act_refs[d]))
        sel = pack_ref[0:LANES, :]
        out.append(mm_nt(high, sel) + mm_nt(low, sel))
    return out


def own_front_kernel(dims, pack_ref, sigs_ref, pos_ref, rem_ref, act0_ref, act1_ref, dsil0_ref, dsil1_ref, part_ref,
                     ext_ref):
    parts = conv_silu(dims, 0, sigs_ref, pack_ref, pos_ref, rem_ref, (act0_ref, act1_ref), (dsil0_ref, dsil1_ref),
                      ext_ref)
    for d in range(2):
        part_ref[d] = parts[d]


def front_kernel(dims, *refs):
    n_ch, n_tok, rows, width, chans, inner, rank, states, taps = dims
    total = rows * n_ch
    nt = chans // LANES
    xd = rank + 2 * states
    packs = refs[:n_ch - 1]
    (sigs_ref, pos_ref, rem_ref, part_ref, stepw_hbm, sbias_hbm, picked_ref, stp0_ref, stp1_ref, sgm0_ref, sgm1_ref,
     ext_ref, stepw_pad_ref, pre_ref, act0_ref, act1_ref, stepw_ref, sbias_ref, sems) = refs[n_ch - 1:]
    stp_refs, sgm_refs = (stp0_ref, stp1_ref), (sgm0_ref, sgm1_ref)
    fetches = fetch_all((stepw_hbm, sbias_hbm), (stepw_ref, sbias_ref), sems)
    picked_ref[...] = part_ref[...]
    for k in range(1, n_ch):
        parts = conv_silu(dims, k, sigs_ref, packs[k - 1], pos_ref, rem_ref, (act0_ref, act1_ref), None, ext_ref)
        for d in range(2):
            picked_ref[d] += parts[d]
    for fetch in fetches:
        fetch.wait()
    stepw_pad_ref[...] = jnp.zeros_like(stepw_pad_ref)
    for d in range(2):
        base = d * xd
        stepw_pad_ref[d, base:base + rank, :] = stepw_ref[d]
        pre_ref[...] = mm3(mm, picked_ref[d], stepw_pad_ref[d]) + sbias_ref[d:d + 1, :]

        def step_rows(r0):
            for lt in range(nt):
                x = pre_ref[pl.ds(r0, BLOCK), tile(lt)]
                tail = jnp.exp(-jnp.abs(x))
                whole = 1.0 + tail
                inv = pltpu.reciprocal(whole, approx=True)
                inv = inv * (2.0 - whole * inv)
                small = tail * (1.0 - tail * (0.5 - tail * (1.0 / 3.0)))
                stp_refs[d][lt, pl.ds(r0, BLOCK), :] = jnp.maximum(x, 0.0) + jnp.where(
                    tail < 1e-3, small, jnp.log(whole)
                )
                sgm_refs[d][lt, pl.ds(r0, BLOCK), :] = jnp.where(x >= 0.0, inv, tail * inv)

        over_rows(total, step_rows)


def conv_rows_of(pack_ref, taps):
    return pack_ref[LANES:LANES + 16, :].astype(F32) + pack_ref[LANES + 16:LANES + 32, :].astype(F32)


def selectors(states):
    lanes = np.arange(states * LANES) >> 7
    column = np.arange(LANES)
    spread = ((column[:, None] % states) == lanes[None, :]) & (column[:, None] < 2 * states)
    gather = lanes[:, None] == column[None, :]
    return jnp.asarray(spread, LOW), jnp.asarray(gather, LOW)


def spread_maps(first, states, picked, lanes_ref, e_ref, dest):
    moved = pltpu.roll(picked, LANES - first, 1)
    high = moved.astype(LOW).astype(F32)
    low = pltpu.roll(moved - high, states, 1)
    spot = lax.broadcasted_iota(jnp.int32, moved.shape, 1)
    lanes_ref[...] = jnp.where(spot < states, high, jnp.where(spot < 2 * states, low, 0.0)).astype(LOW)

    dest[...] = mm(lanes_ref[...], e_ref[...])


def fill_rates(rate, nt, states, r2_ref):
    for lt in range(nt):
        for n in range(states):
            r2_ref[lt, n] = jnp.broadcast_to(rate[n:n + 1, tile(lt)] * LOG2E, (8, LANES))


def gate_kernel(dims, *refs):
    n_ch, n_tok, rows, width, chans, inner, rank, states, taps = dims
    total = rows * n_ch
    cots = refs[:n_ch]
    wout_ref, gate_ref, _, cotp_ref, gg_ref, gy_ref = refs[n_ch:]
    me = lax.axis_index("ch")
    for r0 in range(0, total, 256):
        cotp = 0.0
        for k in range(n_ch):
            moved = order_matrix(r0, 256, lax.rem(me + k, n_ch) * rows, rows, total)
            cotp = cotp + mm(moved, cots[k][...])
        cotp_ref[r0:r0 + 256, :] = cotp.astype(LOW)
    gg_ref[...] = mm_nt(cotp_ref[...], wout_ref[...]).astype(LOW)

    def gate_rows(r0):
        rr = pl.ds(r0, BLOCK)
        for lt in range(chans // LANES):
            gate = gate_ref[rr, tile(lt)].astype(F32)
            gy_ref[lt, rr, :] = gg_ref[rr, tile(lt)].astype(F32) * (gate * sigmoid(gate)) * 0.5

    over_rows(total, gate_rows)


def forward_kernel(dims, d, gy_ref, act_ref, stp_ref, picked_ref, dlog_ref, place_ref, e_ref, er_ref, *refs):
    n_ch, n_tok, rows, width, chans, inner, rank, states, taps = dims
    total = rows * n_ch
    length = total // 8
    nt = chans // LANES
    xd = rank + 2 * states
    first = d * xd + rank
    (y_ref, gains_ref, bb_ref, cb_ref, a_ref, h_ref, gmap_ref,
     r2_ref, lanes_ref, p_ref) = refs
    zero = jnp.zeros((8, LANES), F32)
    fill_rates(-jnp.exp(dlog_ref[d]), nt, states, r2_ref)
    spread_maps(first, states, picked_ref[d], lanes_ref, e_ref, bb_ref)
    spread_maps(first + states, states, picked_ref[d], lanes_ref, e_ref, cb_ref)
    p_ref[...] = jnp.zeros_like(p_ref)

    def along(j):
        return pl.multiple_of((length - 1 - j if d else j) * 8, 8)

    def scan_tile(lt, carry):
        def ends(j2, state):
            state, step_sum = list(state[:-1]), state[-1]
            at = [along(2 * j2 + jj) for jj in range(2)]
            sk, u = [], []
            for r0 in at:
                step = stp_ref[lt, pl.ds(r0, 8), :]
                sk.append(jnp.where(place_ref[pl.ds(r0, 8), :] == 0, HUGE_STEP, step))
                u.append(step * act_ref[lt, pl.ds(r0, 8), :])
            for n in range(states):
                for jj, r0 in enumerate(at):
                    a = jnp.exp2(sk[jj] * r2_ref[lt, n])
                    a_ref[lt, pl.ds(r0, 8), lane(n)] = a
                    state[n] = a * state[n] + u[jj] * bb_ref[pl.ds(r0, 8), lane(n)]
            return tuple(state) + (step_sum + (sk[0] + sk[1]),)

        out = over_pairs(length, ends, (zero,) * (states + 1))
        begin = []
        for n in range(states):
            whole_gain = jnp.exp2(out[-1] * r2_ref[lt, n])
            gains_ref[lt, n] = whole_gain
            begin.append(link_blocks(whole_gain, out[n], d == 0))

        def forward(j2, state):
            state = list(state)
            at = [along(2 * j2 + jj) for jj in range(2)]
            r16 = pl.multiple_of((length - 2 - 2 * j2 if d else 2 * j2) * 8, 16)
            u = [stp_ref[lt, pl.ds(r0, 8), :] * act_ref[lt, pl.ds(r0, 8), :] for r0 in at]
            gy = [gy_ref[lt, pl.ds(r0, 8), :] for r0 in at]
            sums = [[None, None], [None, None]]
            for n in range(states):
                prods = []
                for jj, r0 in enumerate(at):
                    h_ref[lt, pl.ds(r0, 8), lane(n)] = state[n]
                    state[n] = a_ref[lt, pl.ds(r0, 8), lane(n)] * state[n] + u[jj] * bb_ref[pl.ds(r0, 8), lane(n)]
                    term = state[n] * cb_ref[pl.ds(r0, 8), lane(n)]
                    sums[jj][n % 2] = term if sums[jj][n % 2] is None else sums[jj][n % 2] + term
                    prods.append(state[n] * gy[jj])
                p_ref[pl.ds(r16, 16), lane(n)] += jnp.concatenate(prods[::-1] if d else prods, axis=0).astype(LOW)
            for jj, r0 in enumerate(at):
                y_ref[lt, pl.ds(r0, 8), :] = sums[jj][0] + sums[jj][1]
            return tuple(state)

        over_pairs(length, forward, tuple(begin))
        return carry

    lax.fori_loop(0, nt, scan_tile, 0)
    gmap_ref[...] = pltpu.roll(mm(p_ref[...], er_ref[...]), first + states, 1)


def out_kernel(dims, y0_ref, y1_ref, act0_ref, act1_ref, skip_ref, gate_ref, gg_ref, normed_ref, cotp_ref, *refs):
    n_ch, n_tok, rows, width, chans, inner, rank, states, taps = dims
    total = rows * n_ch
    gated_ref, ggate_ref, own_ref, send_ref = refs

    def gate_back(r0):
        rr = pl.ds(r0, BLOCK)
        for lt in range(chans // LANES):
            sl = tile(lt)
            out = (
                y0_ref[lt, rr, :] + y1_ref[lt, rr, :]
                + skip_ref[0:1, sl] * act0_ref[lt, rr, :] + skip_ref[1:2, sl] * act1_ref[lt, rr, :]
            ) * 0.5
            gate = gate_ref[rr, sl].astype(F32)
            sg = sigmoid(gate)
            silu = gate * sg
            gated_ref[rr, sl] = (out * silu).astype(LOW)
            ggate_ref[rr, sl] = (gg_ref[rr, sl].astype(F32) * out * (sg + silu * (1.0 - sg))).astype(LOW)

    over_rows(total, gate_back)
    gated = gated_ref[...]
    gout = mm_tn(gated, cotp_ref[...])
    gin = mm_tn(normed_ref[...], ggate_ref[...])
    folded = [gout[:, i * chans:(i + 1) * chans] for i in range(width // chans)]
    pack(own_ref, send_ref, [folded, [gin]])


def block_kernel(dims, gated_ref, wout_ref, _, own_ref, *refs):
    n_ch, rows = dims[0], dims[2]
    part = mm(gated_ref[...], wout_ref[...])
    token_rows(lax.axis_index("ch"), part, n_ch, rows, rows * n_ch, own_ref, refs)


def token_rows(me, part, n_ch, rows, total, own_ref, other_refs):
    high, low = split(part)
    mine = take_tokens(me * rows, rows, total)
    own_ref[...] = mm(mine, high) + mm(mine, low)
    for k in range(1, n_ch):
        theirs = take_tokens(lax.rem(me + k, n_ch) * rows, rows, total)
        other_refs[k - 1][...] = mm(theirs, high).astype(LOW)


def my_place():
    tok = lax.axis_index("tok")
    return tok & 1, (tok >> 1) & 1


def pack(own_ref, send_ref, groups):
    core, near = my_place()
    runs = []
    at = 0
    for group in groups:
        total = sum(piece.shape[0] for piece in group)
        size = chunk_rows(PIECES, total)
        place = 0
        for piece in group:
            for i in range(0, piece.shape[0], 8):
                runs.append(divmod(place + i, size) + (at, piece[i:i + 8, :]))
            place += piece.shape[0]
        for i in range(place, size * PIECES, 8):
            runs.append(divmod(i, size) + (at, jnp.zeros((8, own_ref.shape[2]), F32)))
        at += size
    for side in range(2):
        @pl.when(core == side)
        def _():
            for p, r, base, rows in runs:
                slot = (p & 1) ^ near
                if p >> 1 == side:
                    own_ref[slot, base + r:base + r + 8, :] = rows
                else:
                    send_ref[slot, base + r:base + r + 8, :] = rows.astype(LOW)


def backward_kernel(dims, d, lt, n_wait, *refs):
    n_ch, n_tok, rows, width, chans, inner, rank, states, taps = dims
    total = rows * n_ch
    length = total // 8
    xd = rank + 2 * states
    base = d * xd
    first = base + rank
    sl = tile(lt)
    last_tile = lt == chans // LANES - 1
    refs = list(refs)

    def take(n):
        out = refs[:n]
        del refs[:n]
        return out

    (gy_ref, act_ref, stp_ref, sgm_ref, picked_ref, gains_ref, bb_ref, cb_ref, a_ref, h_ref, dlog_ref, skip_ref,
     stepw_ref, er_ref) = take(14)
    before = take(2)
    take(n_wait)
    gpick_ref, = take(1)
    if last_tile:
        low_ref, = take(1)
    else:
        q_ref, = take(1)
    gact_ref, gstepw_ref, gdlog_ref, misc_ref = take(4)
    if last_tile:
        q_ref, = take(1)
    r2_ref, gu_ref, gs_ref, gpre_ref, stepw_pad_ref = refs

    rate = -jnp.exp(dlog_ref[d, :, sl])
    for n in range(states):
        r2_ref[n] = jnp.broadcast_to(rate[n:n + 1] * LOG2E, (8, LANES))
    zero = jnp.zeros((8, LANES), F32)

    def against(j):
        return pl.multiple_of((j if d else length - 1 - j) * 8, 8)

    def ends_back(j2, state):
        state = list(state)
        at = [against(2 * j2 + jj) for jj in range(2)]
        gy = [gy_ref[lt, pl.ds(r0, 8), :] for r0 in at]
        for n in range(states):
            for jj, r0 in enumerate(at):
                state[n] = a_ref[lt, pl.ds(r0, 8), lane(n)] * (cb_ref[pl.ds(r0, 8), lane(n)] * gy[jj] + state[n])
        return tuple(state)

    back = over_pairs(length, ends_back, (zero,) * states)
    begin = [link_blocks(gains_ref[lt, n], back[n], d == 1) for n in range(states)]

    def backward(j2, state):
        grad, rate_sum = list(state[:states]), list(state[states:])
        at = [against(2 * j2 + jj) for jj in range(2)]
        r16 = pl.multiple_of((2 * j2 if d else length - 2 - 2 * j2) * 8, 16)
        gy = [gy_ref[lt, pl.ds(r0, 8), :] for r0 in at]
        step = [stp_ref[lt, pl.ds(r0, 8), :] for r0 in at]
        u = [step[jj] * act_ref[lt, pl.ds(r0, 8), :] for jj, r0 in enumerate(at)]
        gu = [[None, None], [None, None]]
        gs = [[None, None], [None, None]]
        for n in range(states):
            prods = []
            for jj, r0 in enumerate(at):
                g = cb_ref[pl.ds(r0, 8), lane(n)] * gy[jj] + grad[n]
                prods.append(g * u[jj])
                term = g * bb_ref[pl.ds(r0, 8), lane(n)]
                gu[jj][n % 2] = term if gu[jj][n % 2] is None else gu[jj][n % 2] + term
                grad[n] = a_ref[lt, pl.ds(r0, 8), lane(n)] * g
                q = grad[n] * h_ref[lt, pl.ds(r0, 8), lane(n)]
                rate_sum[n] = rate_sum[n] + q * step[jj]
                term = q * r2_ref[n]
                gs[jj][n % 2] = term if gs[jj][n % 2] is None else gs[jj][n % 2] + term
            value = jnp.concatenate(prods if d else prods[::-1], axis=0).astype(LOW)
            if lt:
                value = value + before[1][pl.ds(r16, 16), lane(n)]
            q_ref[pl.ds(r16, 16), lane(n)] = value
        for jj, r0 in enumerate(at):
            gu_ref[pl.ds(r0, 8), :] = gu[jj][0] + gu[jj][1]
            gs_ref[pl.ds(r0, 8), :] = gs[jj][0] + gs[jj][1]
        return tuple(grad) + tuple(rate_sum)

    last = over_pairs(length, backward, tuple(begin) + (zero,) * states)
    for n in range(states):
        gdlog_ref[n:n + 1, :] = jnp.sum(last[states + n], axis=0, keepdims=True) * rate[n:n + 1]
    misc_ref[...] = jnp.zeros_like(misc_ref)

    def post_rows(r0):
        rr = pl.ds(r0, BLOCK)
        active = act_ref[lt, rr, :]
        gu = gu_ref[rr, :]
        gy = gy_ref[lt, rr, :]
        gpre = (gs_ref[rr, :] * LN2 + gu * active) * sgm_ref[lt, rr, :]
        gpre_ref[rr, :] = gpre
        gact_ref[rr, :] = gu * stp_ref[lt, rr, :] + skip_ref[d:d + 1, sl] * gy
        misc_ref[0:1, :] += jnp.sum(gpre, axis=0, keepdims=True)
        misc_ref[1:2, :] += jnp.sum(gy * active, axis=0, keepdims=True)

    over_rows(total, post_rows)
    stepw_pad_ref[...] = jnp.zeros_like(stepw_pad_ref)
    stepw_pad_ref[base:base + rank, :] = stepw_ref[d, :, sl]
    gpre = gpre_ref[...]
    gpick = mm3(mm_nt, gpre, stepw_pad_ref[...]) + before[0][...]
    if last_tile:
        gpick = gpick + pltpu.roll(mm(q_ref[...], er_ref[...]), first, 1)
        low_ref[...] = gpick.astype(LOW)
    gpick_ref[...] = gpick
    gstepw_ref[...] = mm3(mm_tn, picked_ref[d], gpre)[base:base + rank, :]


def conv_back(dims, d, pos_ref, rem_ref, gpick_refs, gact_refs, act_ref, dsil_ref, sigs_ref, pack_ref, gsig_ref,
              gsel_ref, gconv_ref, gcp_ref, ext_ref, gcs_ref):
    n_ch, n_tok, rows, width, chans, inner, rank, states, taps = dims
    total = rows * n_ch
    nt = chans // LANES
    halo = 8 * (taps - 1)
    xd = rank + 2 * states
    gpick = gpick_refs[0][...]
    for k in range(1, n_ch):
        gpick = gpick + gpick_refs[k][...].astype(F32)
    spot = lax.broadcasted_iota(jnp.int32, (total, LANES), 1)
    gpick = jnp.where((spot >= d * xd) & (spot < (d + 1) * xd), gpick, 0.0)
    high, low = split(gpick)
    sel = pack_ref[0:LANES, :]
    gcp_ref[pl.ds(halo, total), :] = mm(high, sel) + mm(low, sel)
    gsel_ref[...] = mm3(mm_tn, gpick, wide(act_ref))[d * xd:(d + 1) * xd, :]
    ext_ref[pl.ds(halo, total), :] = sigs_ref[0].astype(F32)
    halo_fill(ext_ref, total, halo, slice(None))
    gcs_ref[...] = jnp.zeros_like(gcs_ref)
    conv = conv_rows_of(pack_ref, taps)

    def fold8(x):
        out = x[0:8]
        for i in range(8, BLOCK, 8):
            out = out + x[i:i + 8]
        return out

    def conv_rows(r0):
        rr = pl.ds(r0, BLOCK)
        inside = rem_ref[rr, :] if d else pos_ref[rr, :]
        for lt in range(nt):
            sl = tile(lt)
            gc = (gcp_ref[pl.ds(r0 + halo, BLOCK), sl] + gact_refs[lt][rr, :]) * dsil_ref[lt, rr, :]
            gcp_ref[pl.ds(r0 + halo, BLOCK), sl] = gc
            gcs_ref[taps, :, sl] += fold8(gc)
            gcs_ref[taps - 1, :, sl] += fold8(gc * ext_ref[pl.ds(r0 + halo, BLOCK), sl])
            for lag in range(1, taps):
                far = ext_ref[pl.ds(r0 + (halo + 8 * lag if d else halo - 8 * lag), BLOCK), sl]
                gcs_ref[taps - 1 - lag, :, sl] += fold8(jnp.where(inside >= lag, gc * far, 0.0))

    over_rows(total, conv_rows)
    halo_fill(gcp_ref, total, halo, slice(None))

    def signal_rows(r0):
        rr = pl.ds(r0, BLOCK)
        inside = pos_ref[rr, :] if d else rem_ref[rr, :]
        for lt in range(nt):
            sl = tile(lt)
            at = d * (taps + 1)
            summed = conv[at + taps - 1:at + taps, sl] * gcp_ref[pl.ds(r0 + halo, BLOCK), sl]
            for lag in range(1, taps):
                far = gcp_ref[pl.ds(r0 + (halo - 8 * lag if d else halo + 8 * lag), BLOCK), sl]
                summed = summed + conv[at + taps - 1 - lag:at + taps - lag, sl] * jnp.where(inside >= lag, far, 0.0)
            gsig_ref[rr, sl] = summed

    over_rows(total, signal_rows)
    gconv_ref[...] = jnp.zeros_like(gconv_ref)
    for k in range(taps + 1):
        gconv_ref[k:k + 1, :] = jnp.sum(gcs_ref[k], axis=0, keepdims=True)


def first_conv_kernel(dims, n_wait, pos_ref, rem_ref, *refs):
    n_ch, nt = dims[0], dims[4] // LANES
    gpicks, gacts, refs = refs[:n_ch], refs[n_ch:n_ch + nt], refs[n_ch + nt:]
    conv_back(dims, 0, pos_ref, rem_ref, gpicks, gacts, *refs[:4], *refs[4 + n_wait:])


def second_conv_kernel(dims, pos_ref, rem_ref, *refs):
    n_ch, n_tok, rows, width, chans, inner, rank, states, taps = dims
    nt = chans // LANES
    refs = list(refs)

    def take(n):
        out = refs[:n]
        del refs[:n]
        return out

    gpicks, gacts, rest, _ = take(n_ch), take(nt), take(4), take(2)
    gsig0_ref, gsel0_ref, gconv0_ref, normed_ref, ggate_ref, xp_ref, win_ref = take(7)
    tiles = [[take(3) for _ in range(nt)] for _ in range(2)]
    (gsig_ref, own_ref, send_ref, gcp_ref, ext_ref, gcs_ref, gsum_ref, gsel_ref, gconv_ref, small_ref, gain_ref) = refs
    conv_back(dims, 1, pos_ref, rem_ref, gpicks, gacts, *rest, gsum_ref, gsel_ref, gconv_ref, gcp_ref, ext_ref,
              gcs_ref)
    me = lax.axis_index("ch")
    gsig = (gsum_ref[...] + gsig0_ref[...]).astype(LOW)
    gsig_ref[...] = gsig
    gn = grad_normed(dims, me, gsig, ggate_ref, win_ref)
    xp = xp_ref[...].astype(F32)
    scale = lax.rsqrt(jnp.mean(xp * xp, axis=1, keepdims=True) + norm_eps)
    ggain = jnp.sum(gn * xp * scale, axis=0, keepdims=True)
    gin = mm_tn(normed_ref[...], gsig)
    places = small_places(dims)
    small_ref[...] = jnp.zeros_like(small_ref)
    xd = rank + 2 * states
    for d in range(2):
        at = places["select"] + d * xd
        small_ref[at:at + xd, :] = (gsel0_ref, gsel_ref)[d][...]
        conv_ref = (gconv0_ref, gconv_ref)[d]
        at = places["taps"] + d * taps
        small_ref[at:at + taps, :] = conv_ref[0:taps, :]
        small_ref[places["bias"] + d:places["bias"] + d + 1, :] = conv_ref[taps:taps + 1, :]
        for lt in range(nt):
            gstepw_ref, gdlog_ref, misc_ref = tiles[d][lt]
            sl = tile(lt)
            at = places["step"] + d * rank
            small_ref[at:at + rank, sl] = gstepw_ref[...]
            at = places["decay"] + d * states
            small_ref[at:at + states, sl] = gdlog_ref[...]
            small_ref[places["sbias"] + d:places["sbias"] + d + 1, sl] = misc_ref[0:1, :]
            small_ref[places["skip"] + d:places["skip"] + d + 1, sl] = misc_ref[1:2, :]
    gain_ref[...] = jnp.zeros_like(gain_ref)
    for i in range(width // chans):
        gain_ref[i:i + 1, :] = ggain[:, i * chans:(i + 1) * chans]
    pack(own_ref, send_ref, [[gin], [gain_ref[...]], [small_ref[...]]])


def grad_normed(dims, me, gsig, ggate_ref, win_ref):
    n_ch, n_tok, rows, width, chans, inner, rank, states, taps = dims
    return mm_nt(gsig, win_ref[:, pl.ds(pl.multiple_of(me * chans, LANES), chans)]) + mm_nt(
        ggate_ref[...], win_ref[:, inner:inner + chans]
    )


def normed_kernel(dims, gsig_ref, ggate_ref, win_ref, *refs):
    n_ch, n_tok, rows, width, chans, inner, rank, states, taps = dims
    blk_refs, gn_own_ref, part_refs = refs[:n_ch - 1], refs[n_ch - 1], refs[n_ch:]
    me = lax.axis_index("ch")
    gn = grad_normed(dims, me, gsig_ref[...], ggate_ref, win_ref)
    token_rows(me, gn, n_ch, rows, rows * n_ch, gn_own_ref, [ref.at[rows:2 * rows] for ref in part_refs])
    for blk_ref, part_ref in zip(blk_refs, part_refs):
        part_ref[0:rows, :] = blk_ref[...]


def small_places(dims):
    n_ch, n_tok, rows, width, chans, inner, rank, states, taps = dims
    places, at = {}, 0
    for name, size in (
        ("select", 2 * (rank + 2 * states)), ("step", 2 * rank), ("decay", 2 * states), ("taps", 2 * taps),
        ("bias", 2), ("sbias", 2), ("skip", 2),
    ):
        places[name] = at
        at += size
    places["end"] = round_up(at, 8)
    return places


def token_kernel(n_ch, at, tok_ref, cot_ref, gain_ref, blk_ref, gn_ref, *refs):
    parts = refs[:n_ch - 1]
    out_ref, gtok_ref, mark_ref = refs[n_ch - 1:]
    mark_ref[...] = jnp.zeros_like(mark_ref)
    tokens = tok_ref[...].astype(F32)
    out = tokens + blk_ref[...]
    gn = gn_ref[...]
    rows = tok_ref.shape[0]
    for part in parts:
        out = out + part[at:at + rows, :].astype(F32)
        gn = gn + part[at + rows:at + 2 * rows, :].astype(F32)
    out_ref[...] = out.astype(LOW)
    scale = lax.rsqrt(jnp.mean(tokens * tokens, axis=1, keepdims=True) + norm_eps)
    unit = tokens * scale
    scaled = gn * gain_ref[...][None, :]
    gtok_ref[...] = cot_ref[...].astype(F32) + scale * (
        scaled - unit * jnp.mean(scaled * unit, axis=1, keepdims=True)
    )


def join_kernel(n_ch, rb, base_ref, *refs):
    others, out_ref = refs[:n_ch - 1], refs[-1]
    out_ref[0:rb, :] = base_ref[0:rb, :]
    mixed = base_ref[rb:rb + 16, :].astype(F32)
    gain = mixed[0:8]
    for c, other in enumerate(others):
        out_ref[(c + 1) * rb:(c + 2) * rb, :] = other[0:rb, :]
        gain = gain + other[rb:rb + 16, :].astype(F32)[0:8]
    at = n_ch * rb
    out_ref[at:at + 16, :] = jnp.concatenate([gain, mixed[8:16]], axis=0).astype(LOW)
    out_ref[at + 16:, :] = base_ref[rb + 16:, :]


def my_pieces():
    core, near = my_place()
    return [(core ^ (k >> 1)) * 2 + (near ^ (k & 1)) for k in range(PIECES)]


def place_columns(dims, every, at, block_ref, gin_hbm, first, sems):
    n_ch, n_tok, rows, width, chans, inner, rank, states, taps = dims
    rb = chunk_rows(PIECES, width)
    me = lax.axis_index("ch")
    copies = []
    for k, piece in enumerate(my_pieces()):
        rr = pl.ds(pl.multiple_of(piece * rb, 8), rb)
        for c in range(n_ch):
            j = lax.rem(me + c, n_ch) * chans
            block_ref[k, :, pl.ds(pl.multiple_of(j, LANES), chans)] = every[k][
                at + c * rb:at + (c + 1) * rb, :
            ].astype(F32)
        copies.append(pltpu.make_async_copy(block_ref.at[k], gin_hbm.at[rr, first:first + inner], sems.at[k]))
        copies[-1].start()
    return copies


def early_result_kernel(dims, every_ref, gin_hbm, gout_hbm, mark_ref, block_ref, gout_ref, sems):
    n_ch, n_tok, rows, width, chans, inner, rank, states, taps = dims
    ra = chunk_rows(PIECES, chans)
    copies = place_columns(dims, [every_ref.at[k] for k in range(PIECES)], ra, block_ref, gin_hbm, inner, sems)
    for k, piece in enumerate(my_pieces()):
        gout_ref[pl.ds(pl.multiple_of(piece * ra, 8), ra), :] = every_ref[k, 0:ra, :].astype(F32)
    mark_ref[...] = jnp.zeros_like(mark_ref)
    copies.append(pltpu.make_async_copy(gout_ref, gout_hbm, sems.at[PIECES]))
    copies[-1].start()
    for copy in copies:
        copy.wait()


def late_result_kernel(dims, *refs):
    every, gin_hbm, refs = refs[:PIECES], refs[PIECES + 1], refs[PIECES + 2:]
    n_ch, n_tok, rows, width, chans, inner, rank, states, taps = dims
    outs, stages, (small_ref, block_ref, sems) = refs[:8], refs[8:16], refs[16:]
    ggain_ref, gtaps_ref, gbias_ref, gsel_ref, gstep_ref, gsbias_ref, gdecay_ref, gskip_ref = stages
    places = small_places(dims)
    rb, rs = chunk_rows(PIECES, width), chunk_rows(PIECES, places["end"])
    at = n_ch * rb
    gain = 0.0
    for k, piece in enumerate(my_pieces()):
        mixed = every[k][at:at + 8 + rs, :].astype(F32)
        small_ref[pl.ds(pl.multiple_of(piece * rs, 8), rs), :] = mixed[8:]
        gain = gain + mixed[0:8]
    ggain_ref[...] = gain[0]
    xd = rank + 2 * states
    for d in range(2):
        for ref, name, size in ((gsel_ref, "select", xd), (gstep_ref, "step", rank), (gdecay_ref, "decay", states),
                                (gtaps_ref, "taps", taps)):
            first = places[name] + d * size
            ref[d] = small_ref[first:first + size, :]
    for ref, name in ((gbias_ref, "bias"), (gsbias_ref, "sbias"), (gskip_ref, "skip")):
        ref[...] = small_ref[places[name]:places[name] + 2, :]
    copies = [pltpu.make_async_copy(a, b, sems.at[PIECES + i]) for i, (a, b) in enumerate(zip(stages, outs))]
    for copy in copies:
        copy.start()
    copies += place_columns(dims, every, 0, block_ref, gin_hbm, 0, sems)
    for copy in copies:
        copy.wait()


def chunk_rows(n_tok, total):
    return round_up(-(-total // n_tok), 8)


def vmem_specs(n):
    return [pl.BlockSpec(memory_space=pltpu.VMEM)] * n


def kernel_call(kernel, name, operands, outs, scratch, limit, us, places=(), hbm_outs=(), aliases=()):
    specs = vmem_specs(len(operands))
    for i, space in places:
        specs[i] = pl.BlockSpec(memory_space=space)
    return pl.pallas_call(
        kernel,
        name=name,
        out_shape=outs,
        in_specs=specs,
        out_specs=[pl.BlockSpec(memory_space=pl.ANY if i in hbm_outs else pltpu.VMEM) for i in range(len(outs))],
        scratch_shapes=scratch,
        input_output_aliases=dict(aliases),
        compiler_params=pltpu.CompilerParams(vmem_limit_bytes=limit * 1024 * 1024),
        cost_estimate=pl.CostEstimate(flops=int(us * 1e7), bytes_accessed=int(us * 3e4), transcendentals=0),
    )(*operands)


def rotated(x, n_ch):
    return [x] + [
        lax.ppermute(x, "ch", [((i + k) % n_ch, i) for i in range(n_ch)]) for k in range(1, n_ch)
    ]


def sent(parts, n_ch):
    return [
        lax.ppermute(parts[k - 1], "ch", [(i, (i + k) % n_ch) for i in range(n_ch)]) for k in range(1, n_ch)
    ]


def partner_pairs(n_tok, stride):
    return [(i, i ^ stride) for i in range(n_tok)]


def swap(x, n_tok, stride):
    return lax.ppermute(x, "tok", partner_pairs(n_tok, stride))


def near_strides():
    return [1, 2]


def far_strides(n_tok):
    strides, s = [], 4
    while s < n_tok:
        strides.append(s)
        s *= 2
    return strides


def add_kernel(halving, last, own_ref, got_ref, *refs):
    send_ref = refs[-1]
    if halving:
        refs[-2][...] = own_ref[0] + got_ref[0].astype(F32)
        send_ref[...] = (own_ref[1] + got_ref[1].astype(F32)).astype(LOW)
    else:
        both = own_ref[...] + got_ref[...].astype(F32)
        send_ref[...] = both.astype(LOW)
        if not last:
            refs[-2][...] = both


class Reduction:
    def __init__(self, own, send, n_tok, limit):
        self.own, self.n_tok, self.limit = own, n_tok, limit
        self.strides = [2] + far_strides(n_tok)
        self.got = swap(send, n_tok, 1)

    def done(self):
        return self.own.dtype == LOW

    def add(self, *wait):
        halving, last = self.own.ndim == 3, not self.strides
        shape = self.own.shape[-2:]
        outs = kernel_call(
            functools.partial(add_kernel, halving, last), "add_kernel", (self.own, self.got, *wait),
            ([] if last else [jax.ShapeDtypeStruct(shape, F32)]) + [jax.ShapeDtypeStruct(shape, LOW)], [], self.limit,
            0.1, [(i, pl.ANY) for i in range(2, 2 + len(wait))],
        )
        self.own = outs[0]
        if not last:
            self.got = swap(outs[1], self.n_tok, self.strides.pop(0))


def stack_kernel(spans, *refs):
    at = 0
    for (first, rows), ref in zip(spans, refs):
        refs[-1][at:at + rows, :] = ref[first:first + rows, :]
        at += rows


def stack(parts, wait, limit):
    parts = [part if isinstance(part, tuple) else (part, 0, part.shape[0]) for part in parts]
    arrays, spans = [part[0] for part in parts], [part[1:] for part in parts]
    shape = (sum(rows for _, rows in spans), arrays[0].shape[1])
    return kernel_call(
        functools.partial(stack_kernel, spans), "stack_kernel", (*arrays, wait), [jax.ShapeDtypeStruct(shape, LOW)], [],
        limit, 0.1, [(len(parts), pl.ANY)],
    )[0]


def local(
    tokens,
    cotangent,
    norm_gain,
    in_proj,
    conv_weight,
    conv_bias,
    select_proj,
    step_proj,
    step_bias,
    decay_log,
    skip_gain,
    out_proj,
    clip_lengths,
):
    n_ch, n_tok = lax.axis_size("ch"), lax.axis_size("tok")
    rows, width = tokens.shape
    real = conv_bias.shape[1]
    taps, rank, states = conv_weight.shape[1], step_proj.shape[1], decay_log.shape[1]
    chans = round_up(real, LANES)
    extra = chans - real
    xd = rank + 2 * states

    def pad_last(x):
        return jnp.pad(x, [(0, 0)] * (x.ndim - 1) + [(0, extra)]) if extra else x

    if extra:
        in_proj = pad_last(in_proj.reshape(width, 2 * n_ch, real)).reshape(width, 2 * n_ch * chans)
        step_proj, step_bias, decay_log, skip_gain = map(pad_last, (step_proj, step_bias, decay_log, skip_gain))
        out_proj = jnp.pad(out_proj, ((0, extra), (0, 0)))
    inner = n_ch * chans
    total = rows * n_ch
    nt = chans // LANES
    span = states * LANES
    halo = 8 * (taps - 1)
    fold = width // chans
    dims = (n_ch, n_tok, rows, width, chans, inner, rank, states, taps)
    limit = 16 if total <= 256 else 60
    shape = jax.ShapeDtypeStruct
    vm = pltpu.VMEM
    one = (nt, total, LANES)
    dma = pltpu.SemaphoreType.DMA
    spot = shape((total, LANES), jnp.int32)

    def far(*arrays):
        return [pltpu.with_memory_space_constraint(x, pltpu.HBM) for x in arrays]

    tok_parts = rotated(tokens, n_ch)
    (packed,) = kernel_call(
        functools.partial(weight_kernel, dims), "weight_kernel",
        far(select_proj.transpose(0, 2, 1), conv_weight, conv_bias), [shape((LANES + 32, chans), LOW)],
        [vm((2, xd, real), F32), vm((2, taps, real), F32), vm((2, real), F32), dma((3,))], limit, 20,
        [(i, pltpu.HBM) for i in range(3)],
    )
    pack_parts = rotated(packed, n_ch)
    fetched = (in_proj, tokens, norm_gain, cotangent)
    win, own, gain, cot_own = kernel_call(
        functools.partial(fetch_kernel, inner, chans), "fetch_kernel", (*far(*fetched), packed),
        [shape((width, inner + chans), LOW)] + [shape(x.shape, x.dtype) for x in fetched[1:]], [dma((5,))], limit, 20,
        [(i, pltpu.HBM) for i in range(len(fetched))] + [(len(fetched), pl.ANY)],
    )
    normed, xp, sigs, gate, pos, rem = kernel_call(
        functools.partial(norm_kernel, dims), "norm_kernel",
        (*far(clip_lengths), own, gain, win, *tok_parts[1:]),
        [shape((total, width), LOW), shape((total, width), LOW), shape((n_ch, total, chans), LOW),
         shape((total, chans), LOW), spot, spot],
        [pltpu.SMEM(clip_lengths.shape, jnp.int32), dma], limit, 50, [(0, pltpu.HBM)],
    )
    cot_parts = rotated(cot_own, n_ch)
    ext = vm((total + 2 * halo, chans), F32)
    act0, act1, dsil0, dsil1, part = kernel_call(
        functools.partial(own_front_kernel, dims), "own_front_kernel", (packed, sigs, pos, rem),
        [shape(one, F32)] * 4 + [shape((2, total, LANES), F32)], [ext], limit, 1,
    )
    picked, stp0, stp1, sgm0, sgm1 = kernel_call(
        functools.partial(front_kernel, dims), "front_kernel",
        (*pack_parts[1:], sigs, pos, rem, part, *far(step_proj, step_bias)),
        [shape((2, total, LANES), F32)] + [shape(one, F32)] * 4,
        [ext, vm((2, LANES, chans), F32), vm((total, chans), F32), vm(one, F32), vm(one, F32),
         vm((2, rank, chans), F32), vm((2, chans), F32), dma((2,))],
        limit, 1, ((n_ch + 3, pltpu.HBM), (n_ch + 4, pltpu.HBM)),
    )

    ra, rb = chunk_rows(PIECES, chans * fold), chunk_rows(PIECES, width)
    r1 = ra + rb
    cotp, gg, gy = kernel_call(
        functools.partial(gate_kernel, dims), "gate_kernel", (*cot_parts, out_proj, gate, picked),
        [shape((total, width), LOW), shape((total, chans), LOW), shape(one, F32)], [], limit, 1,
        [(n_ch + 2, pl.ANY)],
    )
    spread, gather = selectors(states)
    scans = []
    for d, (act, stp) in enumerate(((act0, stp0), (act1, stp1))):
        scans.append(kernel_call(
            functools.partial(forward_kernel, dims, d), "forward_kernel_%d" % d,
            (gy, act, stp, picked, decay_log, rem if d else pos, spread, gather),
            [shape(one, F32), shape((nt, states, 8, LANES), F32)] + [shape((total, span), F32)] * 2
            + [shape((nt, total, span), F32)] * 2 + [shape((total, LANES), F32)],
            [vm((nt, states, 8, LANES), F32), vm((total, LANES), LOW), vm((total, span), LOW)],
            limit, 1,
        ))
    outs = kernel_call(
        functools.partial(out_kernel, dims), "out_kernel",
        (scans[0][0], scans[1][0], act0, act1, skip_gain, gate, gg, normed, cotp),
        [shape((total, chans), LOW), shape((total, chans), LOW), shape((2, r1, chans), F32),
         shape((2, r1, chans), LOW)],
        [], limit, 1,
    )
    gated, ggate, own1, send1 = outs

    early = Reduction(own1, send1, n_tok, limit)
    gpick_parts, gacts, tile_outs = [], [], [[], []]
    for d, (act, stp, sgm) in enumerate(((act0, stp0, sgm0), (act1, stp1, sgm1))):
        gains, bb, cb, decays, before_states, gmap = scans[d][1:]
        before = (gmap, gmap)
        gacts.append([])
        for lt in range(nt):
            final = lt == nt - 1
            operands = (gy, act, stp, sgm, picked, gains, bb, cb, decays, before_states, decay_log, skip_gain,
                        step_proj, gather, *before)
            wait = [early.own] if (d, lt) in ((1, 0), (1, nt - 1)) else []
            outs = kernel_call(
                functools.partial(backward_kernel, dims, d, lt, len(wait)), "backward_kernel_%d%d" % (d, lt),
                (*operands, *wait),
                [shape((total, LANES), F32)]
                + ([shape((total, LANES), LOW)] if final else [shape((total, span), LOW)])
                + [shape((total, LANES), F32), shape((rank, LANES), F32), shape((states, LANES), F32),
                   shape((8, LANES), F32)],
                ([vm((total, span), LOW)] if final else [])
                + [vm((states, 8, LANES), F32), vm((total, LANES), F32), vm((total, LANES), F32),
                   vm((total, LANES), F32), vm((LANES, LANES), F32)],
                limit, 0.5, [(len(operands) + i, pl.ANY) for i in range(len(wait))],
            )
            before = tuple(outs[:2])
            gacts[d].append(outs[2])
            tile_outs[d].extend(outs[-3:])
            if early.strides and (d, lt) in ((0, 0), (0, nt - 1), (1, nt - 2)):
                early.add(outs[-1])
        gpick_parts.append([outs[0]] + rotated(outs[1], n_ch)[1:])

    wait = [tile_outs[1][-1]]
    conv_scratch = [vm((total + 2 * halo, chans), F32), vm((total + 2 * halo, chans), F32),
                    vm((taps + 1, 8, chans), F32)]
    operands = (pos, rem, *gpick_parts[0], *gacts[0], act0, dsil0, sigs, packed, *wait)
    gsig0, gsel0, gconv0 = kernel_call(
        functools.partial(first_conv_kernel, dims, len(wait)), "first_conv_kernel", operands,
        [shape((total, chans), F32), shape((xd, chans), F32), shape((8, chans), F32)],
        conv_scratch, limit, 0.5, [(i, pl.ANY) for i in range(len(operands) - len(wait), len(operands))],
    )
    outs = kernel_call(
        functools.partial(block_kernel, dims), "block_kernel", (gated, out_proj, gconv0),
        [shape((rows, width), F32)] + [shape((rows, width), LOW)] * (n_ch - 1), [], limit, 0.5, [(2, pl.ANY)],
    )
    blk_own, blk_parts = outs[0], outs[1:]
    places = small_places(dims)
    rs = chunk_rows(PIECES, places["end"])
    r2 = rs + rb + 8
    gsig, own2, send2 = kernel_call(
        functools.partial(second_conv_kernel, dims), "second_conv_kernel",
        (pos, rem, *gpick_parts[1], *gacts[1], act1, dsil1, sigs, packed, blk_own, early.got, gsig0, gsel0, gconv0, normed, ggate, xp,
         win, *tile_outs[0], *tile_outs[1]),
        [shape((total, chans), LOW), shape((2, r2, chans), F32), shape((2, r2, chans), LOW)],
        conv_scratch + [vm((total, chans), F32), vm((xd, chans), F32), vm((8, chans), F32),
                        vm((places["end"], chans), F32), vm((8, chans), F32)],
        limit, 0.5, [(6 + n_ch + nt, pl.ANY), (7 + n_ch + nt, pl.ANY)],
    )
    outs = kernel_call(
        functools.partial(normed_kernel, dims), "normed_kernel", (gsig, ggate, win, *blk_parts),
        [shape((rows, width), F32)] + [shape((2 * rows, width), LOW)] * (n_ch - 1), [], limit, 0.5,
    )
    gn_own, token_parts = outs[0], outs[1:n_ch]

    late = Reduction(own2, send2, n_tok, limit)
    early.add(gn_own)
    while not early.done():
        early.add()
    gate = (early.own, ra, rb)
    if n_ch == 2 and width == chans:
        token_got = gates = sent([stack([gate, token_parts[0]], gn_own, limit)], n_ch)
    else:
        token_got, gates = sent(token_parts, n_ch), rotated(early.own[ra:], n_ch)[1:]
    late.add(gn_own)
    late.add()
    block_out, grad_tokens, mark = kernel_call(
        functools.partial(token_kernel, n_ch, token_got[0].shape[0] - 2 * rows), "token_kernel",
        (own, cot_own, gain, blk_own, gn_own, *token_got),
        [shape((rows, width), LOW), shape((rows, width), F32), shape((8, LANES), F32)], [], limit, 0.5,
    )
    early_piece = stack([early.own, *((got, 0, rb) for got in gates)], mark, limit)
    first_got = swap(early_piece, n_tok, 2)
    late.add(mark)
    while not late.done():
        late.add()
    early_pair = stack([early_piece, first_got], late.own, limit).reshape(2, ra + n_ch * rb, chans)
    every1 = jnp.concatenate([early_pair, swap(early_pair, n_tok, 1)], axis=0)
    assert rb % 16 == 0 and (rs + 8) % 16 == 0
    shared = late.own[:rb + 16]
    sides = [[], []]
    for side in range(2):
        for c in range(n_ch):
            if (side, c) == (0, 0):
                sides[0].append(late.own)
                continue
            pairs = [
                ((i ^ (2 * side)) * n_ch + (j + c) % n_ch, i * n_ch + j) for i in range(n_tok) for j in range(n_ch)
            ]
            sides[side].append(lax.ppermute(shared if c else late.own, ("tok", "ch"), pairs))

    def join(wait):
        mine = [
            kernel_call(
                functools.partial(join_kernel, n_ch, rb), "join_kernel", (*parts, wait),
                [shape((n_ch * rb + 8 + rs, chans), LOW)], [], limit, 0.5, [(n_ch, pl.ANY)],
            )[0] for parts in sides
        ]
        return mine + [swap(piece, n_tok, 1) for piece in mine]

    if not extra and fold == 1 and ra * PIECES == chans and rb * PIECES == width:
        block = vm((PIECES, rb, inner), F32)
        gin, gout, mark = kernel_call(
            functools.partial(early_result_kernel, dims), "early_result_kernel", (every1,),
            [shape((width, 2 * inner), F32), shape((chans, width), F32), shape((8, LANES), F32)],
            [block, vm((chans, width), F32), dma((PIECES + 1,))], limit, 2, hbm_outs=(0, 1),
        )
        every2 = join(mark)
        small_shapes = [(width,), (2, taps, chans), (2, chans), (2, xd, chans), (2, rank, chans), (2, chans),
                        (2, states, chans), (2, chans)]
        gin, ggain, gtaps, gbias, gsel, gstep, gsbias, gdecay, gskip = kernel_call(
            functools.partial(late_result_kernel, dims), "late_result_kernel",
            (*every2, gin),
            [shape((width, 2 * inner), F32)] + [shape(x, F32) for x in small_shapes],
            [vm(x, F32) for x in small_shapes] + [vm((rs * PIECES, chans), F32), block, dma((PIECES + 8,))], limit, 2,
            [(PIECES, pl.ANY)], hbm_outs=range(9), aliases={PIECES: 0},
        )
    else:
        every2 = jnp.stack(join(late.own))
        me, tok = lax.axis_index("ch"), lax.axis_index("tok")
        mine = (tok & 1) * 2 + ((tok >> 1) & 1)
        at = jnp.arange(PIECES) ^ mine
        every1, every2 = every1[at], every2[at]
        turn = (jnp.arange(n_ch) - me) % n_ch
        gate = every1[:, ra:].reshape(PIECES, n_ch, rb, chans)
        signal = every2[:, :n_ch * rb].reshape(PIECES, n_ch, rb, chans)
        gin = jnp.concatenate([signal[:, turn], gate[:, turn]], axis=1).transpose(0, 2, 1, 3)[..., :real]
        gin = gin.reshape(PIECES * rb, 2 * n_ch * real)[:width].astype(F32)
        gout = every1[:, :ra].reshape(PIECES * ra, chans)[:chans * fold]
        gout = jnp.concatenate([gout[i * chans:(i + 1) * chans] for i in range(fold)], axis=1)[:real].astype(F32)
        small = every2[:, n_ch * rb + 8:].reshape(PIECES * rs, chans).astype(F32)
        ggain = jnp.sum(every2[:, n_ch * rb:n_ch * rb + 8].astype(F32), axis=0)[:fold].reshape(width)

        def rows_of(name, size):
            return small[places[name]:places[name] + size]

        gsel, gstep, gdecay, gtaps = (
            rows_of(name, 2 * size).reshape(2, size, chans)[..., :real]
            for name, size in (("select", xd), ("step", rank), ("decay", states), ("taps", taps))
        )
        gbias, gsbias, gskip = (rows_of(name, 2)[:, :real] for name in ("bias", "sbias", "skip"))
    return (
        block_out,
        grad_tokens,
        ggain,
        gin,
        gtaps,
        gbias,
        gsel.transpose(0, 2, 1),
        gstep,
        gsbias,
        gdecay,
        gskip,
        gout,
    )


def solution(mesh):
    return jax.shard_map(
        local,
        mesh=mesh,
        in_specs=(
            P(("tok", "ch"), None),
            P(("tok", "ch"), None),
            P(),
            P(),
            P(None, None, "ch"),
            P(None, "ch"),
            P(None, "ch", None),
            P(None, None, "ch"),
            P(None, "ch"),
            P(None, None, "ch"),
            P(None, "ch"),
            P("ch", None),
            P("tok", None),
        ),
        out_specs=(
            P(("tok", "ch"), None),
            P(("tok", "ch"), None),
            P(),
            P(),
            P(None, None, "ch"),
            P(None, "ch"),
            P(None, "ch", None),
            P(None, None, "ch"),
            P(None, "ch"),
            P(None, None, "ch"),
            P(None, "ch"),
            P("ch", None),
        ),
        check_vma=False,
    )
```
